32 devices in a mesh: ctx: 8 (over z, x), tp: 4 (over y, core).
Axes of the slice: x: 2, y: 2, z: 4, core: 2. Of those that a mesh axis runs over, the one named last changes fastest.
Arguments:
- queries: bfloat16 [2048, 2560], P('ctx', 'tp'), may hold values from -6 to 6
- keys: bfloat16 [2048, 512], P('ctx', 'tp'), may hold values from -6 to 6
- values: bfloat16 [2048, 512], P('ctx', 'tp'), may hold values from -6 to 6
- out_weight: bfloat16 [2560, 5120], P('tp'), may hold values from -0.125 to 0.125
- cotangent: bfloat16 [2048, 5120], P('ctx', 'tp'), may hold values from -6 to 6
- doc_ids: int32 [16], replicated, may hold values from 0 to 3, never falling along the last dimension, each value on 1 to 8 neighbouring positions
Outputs:
- mixed: bfloat16 [2048, 5120], P('ctx', 'tp')
- grad_queries: bfloat16 [2048, 2560], P('ctx', 'tp')
- keys_gradient: bfloat16 [2048, 512], P('ctx', 'tp')
- values_gradient: bfloat16 [2048, 512], P('ctx', 'tp')
The draws below stay inside these ranges and needn't reach their ends.
Inputs may be any that keep to these rules, and one draw needn't show every extreme that they name: `doc_ids`: ids never fall from one block to the next; each document covers 1 to 8 blocks and one covers exactly 8.
All inputs are finite; a program needn't handle non-finite values.
Results may differ from the reference program's by a relative error of at most 0.033.
Values may be sent and summed in bfloat16 or wider, within the bound.
No kernel may reach another device: no remote copies, remote signals or barrier semaphores. Data moves between devices by JAX's collectives and lax.ppermute only.
A program may use at most 128 MiB of HBM per device.

```python
import math
import jax
import jax.numpy as jnp
import numpy as np
from jax import lax

D = 5120
HEAD_SIZE = 128
QUERY_HEADS = 20
KEY_VALUE_HEADS = 4
BLK = 128
PACKED_TOKENS = 2048
NBLK = 16
DOC_MOST = 8
DOCS = 4


def draw_queries(key, part):
    random_seed_key = jax.random.fold_in(key, 11)
    return jnp.clip(jax.random.normal(random_seed_key, (PACKED_TOKENS, QUERY_HEADS * HEAD_SIZE), jnp.float32), -6.0, 6.0).astype(jnp.bfloat16)


def draw_keys(key, part):
    random_seed_key = jax.random.fold_in(key, 13)
    return jnp.clip(jax.random.normal(random_seed_key, (PACKED_TOKENS, KEY_VALUE_HEADS * HEAD_SIZE), jnp.float32), -6.0, 6.0).astype(jnp.bfloat16)


def steps_of(stream_key, shape, cuts, low, high):
    def one(dim, blocks):
        draws = jax.random.uniform(jax.random.fold_in(jax.random.fold_in(stream_key, 6), dim), (blocks,), jnp.float32, low / len(cuts), high / len(cuts))
        return jnp.repeat(jnp.exp(draws), shape[dim] // blocks).reshape((-1,) + (1,) * (len(shape) - dim - 1))

    gain = one(*cuts[0])
    for cut in cuts[1:]:
        gain = gain * one(*cut)
    return gain


def profile(number_of, total, most, skew):
    weights = [(1 << 20) // math.isqrt(rank ** skew) + 1 for rank in range(2, number_of + 1)]
    spare, holding = total - most - (number_of - 1), [1] * (number_of - 1)
    while spare > 0:
        movable = [i for i in range(number_of - 1) if holding[i] < most]
        whole, budget = sum([weights[i] for i in movable]), spare
        for i in movable:
            extra = min(most - holding[i], max(1, budget * weights[i] // whole), spare)
            holding[i] = holding[i] + extra
            spare = spare - extra
    return np.array([most] + holding)


def uneven_parts(stream_key, amount, total, limit, slope):
    if amount == 2:
        one = jax.random.randint(stream_key, (), max(1, total - limit), min(limit, total - 1) + 1)
        return jnp.stack([one, total - one])
    lengths = jnp.asarray(profile(amount, total, limit, slope), jnp.int32)
    pairs = (amount - 1) // 2
    donor, sink = lengths[1:1 + 2 * pairs:2], lengths[2:2 + 2 * pairs:2]
    margin = jnp.minimum(donor - 1, limit - sink)
    passed = jax.random.randint(jax.random.fold_in(stream_key, 1), (pairs,), 0, 1 << 20) % (margin + 1)
    lengths = lengths.at[1:1 + 2 * pairs:2].set(donor - passed).at[2:2 + 2 * pairs:2].set(sink + passed)
    return lengths[jax.random.permutation(jax.random.fold_in(stream_key, 2), amount)]


def normal_values(key, extent, scale, bound, pieces=(), held_as=jnp.bfloat16):
    entries = jax.random.normal(key, extent, jnp.float32) * scale
    if len(pieces) > 0:
        entries = steps_of(key, extent, pieces, -0.22, 0.18) * entries
    return jnp.clip(entries, min=-bound, max=bound).astype(held_as)


def setup_inputs(seed: int = 0) -> dict:
    splits = jax.random.split(jax.random.key(seed), 7)
    return {
        "queries": draw_queries(jax.random.fold_in(splits[6], 71), 0),
        "keys": draw_keys(jax.random.fold_in(splits[6], 71), 0),
        "values": normal_values(splits[2], (PACKED_TOKENS, KEY_VALUE_HEADS * HEAD_SIZE), 1.0, 6.0, ((0, 8), (1, 4))),
        "out_weight": normal_values(splits[3], (QUERY_HEADS * HEAD_SIZE, D), (QUERY_HEADS * HEAD_SIZE) ** -0.5, 0.125, ((0, 4),)),
        "cotangent": normal_values(splits[4], (PACKED_TOKENS, D), 1.0, 6.0, ((0, 8), (1, 4))),
        "doc_ids": jnp.searchsorted(jnp.cumsum(uneven_parts(splits[5], DOCS, NBLK, DOC_MOST, 2)), jnp.arange(NBLK), side="right").astype(jnp.int32),
    }


NEG_FILL = -1e+30

def reference(queries, keys, values, out_weight, cotangent, doc_ids):
    query_group_width = QUERY_HEADS // KEY_VALUE_HEADS
    score_scale = 1.0 / math.sqrt(HEAD_SIZE)
    query_tile_block = math.gcd(PACKED_TOKENS, 512)
    block_count = PACKED_TOKENS // query_tile_block
    window = min(PACKED_TOKENS, DOC_MOST * BLK + query_tile_block)
    key_single_precision = keys.astype(jnp.float32).reshape(PACKED_TOKENS, KEY_VALUE_HEADS, HEAD_SIZE)
    value_single_precision = values.astype(jnp.float32).reshape(PACKED_TOKENS, KEY_VALUE_HEADS, HEAD_SIZE)
    token_docs = jnp.repeat(doc_ids, BLK, total_repeat_length=PACKED_TOKENS)
    attention_gradient = jnp.dot(cotangent, out_weight.T, preferred_element_type=jnp.float32).astype(jnp.bfloat16)

    def one_block(running, block_index):
        key_sum, value_sum = running
        leading_row = block_index * query_tile_block
        key_start = jnp.clip(leading_row + query_tile_block - window, 0, PACKED_TOKENS - window).astype(jnp.int32)
        key_all = lax.dynamic_slice_in_dim(key_single_precision, key_start, window, 0)
        value_all = lax.dynamic_slice_in_dim(value_single_precision, key_start, window, 0)
        key_pos = key_start + jnp.arange(window, dtype=jnp.int32)
        key_docs = lax.dynamic_slice_in_dim(token_docs, key_start, window, 0)
        query_row_slab = lax.dynamic_slice_in_dim(queries, leading_row, query_tile_block, 0).astype(jnp.float32).reshape(query_tile_block, KEY_VALUE_HEADS, query_group_width, HEAD_SIZE)
        gradient_rows = lax.dynamic_slice_in_dim(attention_gradient, leading_row, query_tile_block, 0).astype(jnp.float32).reshape(query_tile_block, KEY_VALUE_HEADS, query_group_width, HEAD_SIZE)
        query_pos = leading_row + jnp.arange(query_tile_block, dtype=jnp.int32)
        query_docs = lax.dynamic_slice_in_dim(token_docs, leading_row, query_tile_block, 0)
        allowed = (query_docs[:, None] == key_docs[None, :]) & (key_pos[None, :] <= query_pos[:, None])
        scores = jnp.einsum('tkgd,ukd->kgtu', query_row_slab, key_all) * score_scale
        scores = jnp.where(allowed, scores, NEG_FILL)
        row_top = lax.optimization_barrier(jnp.max(scores, axis=-1, keepdims=True))
        row_total = lax.optimization_barrier(jnp.sum(jnp.where(allowed, jnp.exp(scores - row_top), 0.0), axis=-1, keepdims=True))
        lse = row_top + jnp.log(row_total)
        probs = jnp.where(allowed, jnp.exp(scores - lse), 0.0)
        weights = lax.optimization_barrier(probs.astype(jnp.bfloat16)).astype(jnp.float32)
        attn = jnp.einsum('kgtu,ukd->tkgd', weights, value_all).astype(jnp.bfloat16)
        attn_wide = lax.optimization_barrier(attn).astype(jnp.float32)
        delta = jnp.transpose(lax.optimization_barrier(jnp.sum(gradient_rows * attn_wide, axis=-1)), (1, 2, 0))
        value_add = jnp.einsum('kgtu,tkgd->ukd', weights, gradient_rows)
        prob_grad = jnp.einsum('tkgd,ukd->kgtu', gradient_rows, value_all)
        score_grad = lax.optimization_barrier((probs * (prob_grad - delta[..., None])).astype(jnp.bfloat16)).astype(jnp.float32)
        query_grad = jnp.einsum('kgtu,ukd->tkgd', score_grad, key_all) * score_scale
        key_add = jnp.einsum('kgtu,tkgd->ukd', score_grad, query_row_slab) * score_scale
        key_old = lax.dynamic_slice_in_dim(key_sum, key_start, window, 0)
        value_old = lax.dynamic_slice_in_dim(value_sum, key_start, window, 0)
        key_sum = lax.dynamic_update_slice_in_dim(key_sum, key_old + key_add, key_start, 0)
        value_sum = lax.dynamic_update_slice_in_dim(value_sum, value_old + value_add, key_start, 0)
        outputs = (attn.reshape(query_tile_block, QUERY_HEADS * HEAD_SIZE), query_grad.reshape(query_tile_block, QUERY_HEADS * HEAD_SIZE).astype(jnp.bfloat16))
        return ((key_sum, value_sum), outputs)
    initial_sums = (jnp.zeros((PACKED_TOKENS, KEY_VALUE_HEADS, HEAD_SIZE), jnp.float32), jnp.zeros((PACKED_TOKENS, KEY_VALUE_HEADS, HEAD_SIZE), jnp.float32))
    running_sums, stacked = lax.scan(one_block, initial_sums, jnp.arange(block_count, dtype=jnp.int32))
    attn_all = stacked[0].reshape(PACKED_TOKENS, QUERY_HEADS * HEAD_SIZE)
    grad_queries = stacked[1].reshape(PACKED_TOKENS, QUERY_HEADS * HEAD_SIZE)
    mixed = jnp.dot(attn_all, out_weight, preferred_element_type=jnp.float32).astype(jnp.bfloat16)
    keys_gradient = running_sums[0].reshape(PACKED_TOKENS, KEY_VALUE_HEADS * HEAD_SIZE).astype(jnp.bfloat16)
    values_gradient = running_sums[1].reshape(PACKED_TOKENS, KEY_VALUE_HEADS * HEAD_SIZE).astype(jnp.bfloat16)
    return (mixed, grad_queries, keys_gradient, values_gradient)
```

```python
import functools
import math

import jax
import jax.numpy as jnp
from jax import lax
from jax.experimental import pallas as pl
from jax.experimental.pallas import tpu as pltpu
from jax.sharding import PartitionSpec as P

HEAD_SIZE = 128
BLK = 128
SCALE = 1.0 / math.sqrt(HEAD_SIZE)
SCALE2 = SCALE * math.log2(math.e)
LOW = -1e30
HIGH = 1e30
VMEM_LIMIT = 48 * 1024 * 1024

VMEM = pl.BlockSpec(memory_space=pltpu.VMEM)
SMEM = pl.BlockSpec(memory_space=pltpu.SMEM)


def dot(a, b):
    return jnp.dot(a, b, preferred_element_type=jnp.float32)


def shift(array, axis, by):
    devices = lax.axis_size(axis)
    pairs = [(i, i + by) for i in range(devices) if 0 <= i + by < devices]
    return lax.ppermute(array, axis, pairs)


def swap(array, bit):
    return lax.ppermute(array, "tp", [(i, i ^ bit) for i in range(lax.axis_size("tp"))])


def block(i, n=1):
    return pl.ds(i * BLK, n * BLK)


def allowed(doc_ref, key_block, query_block):
    return (key_block >= 0) & (doc_ref[jnp.maximum(key_block, 0)] == doc_ref[query_block])


def causal(width):
    key = lax.broadcasted_iota(jnp.int32, (BLK, width), 0)
    query = lax.broadcasted_iota(jnp.int32, (BLK, width), 1) % BLK
    return key <= query


def forward_kernel(window, blocks, doc_ref, q_ref, *refs):
    kv_refs = refs[:-8]
    attn_ref, qt_ref, ot_ref, lse_ref, k_all, vt_all, s_all, p_all = refs[-8:]
    heads = q_ref.shape[1] // HEAD_SIZE
    first = lax.axis_index("ctx") * blocks
    at = 0
    for ref in kv_refs:
        rows = ref.shape[0]
        k_all[pl.ds(at, rows), :] = ref[:, :HEAD_SIZE]
        vt_all[:, pl.ds(at, rows)] = ref[:, HEAD_SIZE:].T
        at += rows
    for b in range(blocks):
        for h in range(heads):
            qt_ref[block(b), block(h)] = q_ref[block(b), block(h)].T
        qt = qt_ref[block(b), :]
        width = qt.shape[1]
        top = jnp.full((1, width), LOW, jnp.float32)
        ok = [allowed(doc_ref, first + b - (window - 1) + w, first + b) for w in range(window)]
        for w in range(window):
            s = dot(k_all[block(b + w), :], qt) * SCALE2
            if w == window - 1:
                s = jnp.where(causal(width), s, LOW)
            s_all[block(w), :] = s
            top = jnp.maximum(top, jnp.max(s, axis=0, keepdims=True) + jnp.where(ok[w], 0.0, LOW))
        total = jnp.zeros((1, width), jnp.float32)
        for w in range(window):
            p = jnp.exp2(s_all[block(w), :] - jnp.where(ok[w], top, HIGH))
            total += jnp.sum(p, axis=0, keepdims=True)
            p_all[block(w), :] = p.astype(jnp.bfloat16)
        out = dot(vt_all[:, block(b, window)], p_all[...]) / total
        ot_ref[block(b), :] = out.astype(jnp.bfloat16)
        lse_ref[pl.ds(b, 1), :] = top + jnp.log2(total)
        for h in range(heads):
            attn_ref[block(b), block(h)] = out[:, h * BLK:(h + 1) * BLK].T.astype(jnp.bfloat16)


def forward(doc_ids, q, kvs, window):
    rows, width = q.shape
    blocks = rows // BLK
    held = (window - 1 + blocks) * BLK
    return pl.pallas_call(
        functools.partial(forward_kernel, window, blocks),
        out_shape=[
            jax.ShapeDtypeStruct((rows, width), jnp.bfloat16),
            jax.ShapeDtypeStruct((rows, width), jnp.bfloat16),
            jax.ShapeDtypeStruct((rows, width), jnp.bfloat16),
            jax.ShapeDtypeStruct((blocks, width), jnp.float32),
        ],
        in_specs=[SMEM] + [VMEM] * (1 + len(kvs)),
        out_specs=[VMEM] * 4,
        scratch_shapes=[
            pltpu.VMEM((held, HEAD_SIZE), jnp.bfloat16),
            pltpu.VMEM((HEAD_SIZE, held), jnp.bfloat16),
            pltpu.VMEM((window * BLK, width), jnp.float32),
            pltpu.VMEM((window * BLK, width), jnp.bfloat16),
        ],
        compiler_params=pltpu.CompilerParams(vmem_limit_bytes=VMEM_LIMIT),
        cost_estimate=pl.CostEstimate(
            flops=4 * rows * width * window * BLK * 2, bytes_accessed=2 * 2**20, transcendentals=0
        ),
        name="forward",
    )(doc_ids, q, *kvs)


def backward_kernel(window, blocks, doc_ref, q_ref, qt_ref, ot_ref, lse_ref, g_ref, *refs):
    n = (len(refs) - 10) // 2
    kv_refs, dkv_refs = refs[:n], refs[n + 1:2 * n + 1]
    dq_ref = refs[n]
    k_all, kt_all, v_all, q_rows, g_rows, gt, p_all, ds_all, dk_all = refs[2 * n + 1:]
    heads = q_ref.shape[1] // HEAD_SIZE
    width = q_ref.shape[1]
    first = lax.axis_index("ctx") * blocks
    at = 0
    for ref in kv_refs:
        rows = ref.shape[0]
        k_all[pl.ds(at, rows), :] = ref[:, :HEAD_SIZE]
        kt_all[:, pl.ds(at, rows)] = ref[:, :HEAD_SIZE].T
        v_all[pl.ds(at, rows), :] = ref[:, HEAD_SIZE:]
        at += rows
    dk_all[...] = jnp.zeros_like(dk_all)
    for b in range(blocks):
        for h in range(heads):
            g = g_ref[block(b), block(h)]
            q_rows[block(h), :] = q_ref[block(b), block(h)]
            g_rows[block(h), :] = g
            gt[:, block(h)] = g.T
        qt = qt_ref[block(b), :]
        delta = jnp.sum(
            gt[...].astype(jnp.float32) * ot_ref[block(b), :].astype(jnp.float32),
            axis=0, keepdims=True,
        )
        lse = lse_ref[pl.ds(b, 1), :]
        for w in range(window):
            ok = allowed(doc_ref, first + b - (window - 1) + w, first + b)
            s = dot(k_all[block(b + w), :], qt) * SCALE2
            if w == window - 1:
                s = jnp.where(causal(width), s, LOW)
            p = jnp.exp2(s - jnp.where(ok, lse, HIGH))
            p_all[block(w), :] = p.astype(jnp.bfloat16)
            dp = dot(v_all[block(b + w), :], gt[...])
            ds_all[block(w), :] = (p * (dp - delta)).astype(jnp.bfloat16)
        dk_all[block(b, window), :HEAD_SIZE] += dot(ds_all[...], q_rows[...]) * SCALE
        dk_all[block(b, window), HEAD_SIZE:] += dot(p_all[...], g_rows[...])
        dqt = dot(kt_all[:, block(b, window)], ds_all[...]) * SCALE
        for h in range(heads):
            dq_ref[block(b), block(h)] = dqt[:, h * BLK:(h + 1) * BLK].T.astype(jnp.bfloat16)
    at = 0
    for ref in dkv_refs:
        rows = ref.shape[0]
        ref[...] = dk_all[pl.ds(at, rows), :].astype(ref.dtype)
        at += rows


def backward(doc_ids, q, qt, ot, lse, g, kvs, window):
    rows, width = q.shape
    blocks = rows // BLK
    held = (window - 1 + blocks) * BLK
    types = [jnp.bfloat16] * (len(kvs) - 1) + [jnp.float32]
    return pl.pallas_call(
        functools.partial(backward_kernel, window, blocks),
        out_shape=[jax.ShapeDtypeStruct((rows, width), jnp.bfloat16)]
        + [jax.ShapeDtypeStruct(kv.shape, t) for kv, t in zip(kvs, types)],
        in_specs=[SMEM] + [VMEM] * (5 + len(kvs)),
        out_specs=[VMEM] * (1 + len(kvs)),
        scratch_shapes=[
            pltpu.VMEM((held, HEAD_SIZE), jnp.bfloat16),
            pltpu.VMEM((HEAD_SIZE, held), jnp.bfloat16),
            pltpu.VMEM((held, HEAD_SIZE), jnp.bfloat16),
            pltpu.VMEM((width, HEAD_SIZE), jnp.bfloat16),
            pltpu.VMEM((width, HEAD_SIZE), jnp.bfloat16),
            pltpu.VMEM((HEAD_SIZE, width), jnp.bfloat16),
            pltpu.VMEM((window * BLK, width), jnp.bfloat16),
            pltpu.VMEM((window * BLK, width), jnp.bfloat16),
            pltpu.VMEM((held, 2 * HEAD_SIZE), jnp.float32),
        ],
        compiler_params=pltpu.CompilerParams(vmem_limit_bytes=VMEM_LIMIT),
        cost_estimate=pl.CostEstimate(
            flops=10 * rows * width * window * BLK * 2, bytes_accessed=4 * 2**20, transcendentals=0
        ),
        name="backward",
    )(doc_ids, q, qt, ot, lse, g, *kvs)


def features_in_kernel(ids_ref, *refs):
    *cots, w_ref, out_ref, total = refs
    step = pl.program_id(0)
    base = None
    if len(cots) == 3:
        base, cots = cots[2], cots[:2]

    @pl.when(step == 0)
    def _():
        part = lax.dot_general(
            cots[0][...], w_ref[...], (((1,), (1,)), ((), ())), preferred_element_type=jnp.float32
        )
        total[...] = part if base is None else part + base[...]

    @pl.when(step == 1)
    def _():
        out_ref[...] = (
            total[...]
            + lax.dot_general(
                cots[1][...], w_ref[...], (((1,), (1,)), ((), ())),
                preferred_element_type=jnp.float32,
            )
        ).astype(out_ref.dtype)


def features_in(ids, cots, weight, base, dtype):
    rows, part = cots[0].shape
    depth = weight.shape[0]
    extra = [] if base is None else [base]
    whole = lambda j, ids: (0, 0)
    return pl.pallas_call(
        features_in_kernel,
        out_shape=jax.ShapeDtypeStruct((rows, depth), dtype),
        grid_spec=pltpu.PrefetchScalarGridSpec(
            num_scalar_prefetch=1,
            grid=(2,),
            in_specs=[pl.BlockSpec((rows, part), whole)] * 2
            + [pl.BlockSpec((rows, depth), whole)] * len(extra)
            + [pl.BlockSpec((depth, part), lambda j, ids: (0, ids[j]))],
            out_specs=pl.BlockSpec((rows, depth), whole),
            scratch_shapes=[pltpu.VMEM((rows, depth), jnp.float32)],
        ),
        compiler_params=pltpu.CompilerParams(vmem_limit_bytes=VMEM_LIMIT),
        cost_estimate=pl.CostEstimate(
            flops=4 * rows * part * depth, bytes_accessed=5 * 2**20, transcendentals=0
        ),
        name="features_in",
    )(ids, *cots, *extra, weight)


def features_out_kernel(ids_ref, attn_ref, *refs):
    *extra, w_ref, out_ref = refs
    total = dot(attn_ref[...], w_ref[...])
    for ref in extra:
        total = total + ref[...].astype(jnp.float32)
    out_ref[...] = total.astype(out_ref.dtype)


def features_out(ids, which, attn, weight, part, extra=(), dtype=jnp.bfloat16):
    rows, depth = attn.shape
    tiles = 2
    tile = part // tiles
    return pl.pallas_call(
        features_out_kernel,
        out_shape=jax.ShapeDtypeStruct((rows, part), dtype),
        grid_spec=pltpu.PrefetchScalarGridSpec(
            num_scalar_prefetch=1,
            grid=(tiles,),
            in_specs=[pl.BlockSpec((rows, depth), lambda j, ids: (0, 0))]
            + [pl.BlockSpec((rows, tile), lambda j, ids: (0, j))] * len(extra)
            + [pl.BlockSpec((depth, tile), lambda j, ids: (0, ids[which] * tiles + j))],
            out_specs=pl.BlockSpec((rows, tile), lambda j, ids: (0, j)),
        ),
        compiler_params=pltpu.CompilerParams(vmem_limit_bytes=VMEM_LIMIT),
        cost_estimate=pl.CostEstimate(
            flops=2 * rows * part * depth, bytes_accessed=3 * 2**20, transcendentals=0
        ),
        name="features_out",
    )(ids, attn, *extra, weight)


def on_device(queries, keys, values, out_weight, cotangent, doc_ids):
    rows = queries.shape[0]
    part = cotangent.shape[1]
    ctx_count = lax.axis_size("ctx")
    blocks = rows // BLK
    window = min(8 * blocks, blocks * ctx_count // 2)
    needs = []
    left = window - 1
    while left > 0:
        needs.append(min(left, blocks))
        left -= needs[-1]
    me = lax.axis_index("tp")
    ids = jnp.stack([me, me ^ 1, me ^ 2, me ^ 3]).astype(jnp.int32)

    cot_y = swap(cotangent, 2)
    key_value = jnp.concatenate([keys, values], axis=1)
    kvs = [shift(key_value[rows - n * BLK:], "ctx", s + 1) for s, n in enumerate(needs)]
    kvs = kvs[::-1] + [key_value]
    cot_c = swap(cotangent, 1)
    near = features_in(ids[:2], [cotangent, cot_c], out_weight, None, jnp.float32)
    attn, qt, ot, lse = forward(doc_ids, queries, kvs, window)
    out_a = features_out(ids, 3, attn, out_weight, part)
    out_b = features_out(ids, 2, attn, out_weight, part, [swap(out_a, 1)])
    from_y = swap(out_b, 2)
    out_c = features_out(ids, 1, attn, out_weight, part)
    out_d = features_out(ids, 0, attn, out_weight, part, [swap(out_c, 1)], jnp.float32)

    grad_attn = features_in(ids[2:], [cot_y, swap(cot_y, 1)], out_weight, near, jnp.bfloat16)
    dq, *dkvs = backward(doc_ids, queries, qt, ot, lse, grad_attn, kvs, window)
    own = dkvs[-1]
    for s, (n, dkv) in enumerate(zip(needs, dkvs[-2::-1])):
        back = shift(dkv, "ctx", -(s + 1)).astype(jnp.float32)
        if n < blocks:
            back = jnp.pad(back, ((rows - n * BLK, 0), (0, 0)))
        own = own + back
    mixed = (out_d + from_y.astype(jnp.float32)).astype(jnp.bfloat16)
    return (
        mixed,
        dq,
        own[:, :HEAD_SIZE].astype(jnp.bfloat16),
        own[:, HEAD_SIZE:].astype(jnp.bfloat16),
    )


def solution(mesh):
    return jax.shard_map(
        on_device,
        mesh=mesh,
        in_specs=(
            P("ctx", "tp"),
            P("ctx", "tp"),
            P("ctx", "tp"),
            P("tp", None),
            P("ctx", "tp"),
            P(),
        ),
        out_specs=(P("ctx", "tp"), P("ctx", "tp"), P("ctx", "tp"), P("ctx", "tp")),
        check_vma=False,
    )
```

```python
import functools
import math

import jax
import jax.numpy as jnp
from jax import lax
from jax.experimental import pallas as pl
from jax.experimental.pallas import tpu as pltpu
from jax.sharding import PartitionSpec as P

HEAD_SIZE = 128
BLK = 128
SCALE = 1.0 / math.sqrt(HEAD_SIZE)
SCALE2 = SCALE * math.log2(math.e)
LOW = -1e30
HIGH = 1e30
VMEM_LIMIT = 16 * 1024 * 1024

COST = pl.CostEstimate(flops=2**20, bytes_accessed=2**10, transcendentals=0)
LONG = pl.CostEstimate(flops=2**31, bytes_accessed=2**10, transcendentals=0)

HBM = pl.BlockSpec(memory_space=pltpu.HBM)
VMEM = pl.BlockSpec(memory_space=pltpu.VMEM)
SMEM = pl.BlockSpec(memory_space=pltpu.SMEM)


def in_hbm(array):
    return pltpu.with_memory_space_constraint(array, pltpu.HBM)


def dot(a, b):
    return jnp.dot(a, b, preferred_element_type=jnp.float32)


def shift(array, axis, by):
    devices = lax.axis_size(axis)
    pairs = [(i, i + by) for i in range(devices) if 0 <= i + by < devices]
    return lax.ppermute(array, axis, pairs)


def swap(array, bit, axis="tp"):
    return lax.ppermute(array, axis, [(i, i ^ bit) for i in range(lax.axis_size(axis))])


def block(i, n=1):
    return pl.ds(i * BLK, n * BLK)


def allowed(doc_ref, key_block, query_block):
    return (key_block >= 0) & (doc_ref[jnp.maximum(key_block, 0)] == doc_ref[query_block])


def causal(width):
    key = lax.broadcasted_iota(jnp.int32, (BLK, width), 0)
    query = lax.broadcasted_iota(jnp.int32, (BLK, width), 1) % BLK
    return key <= query


def forward_kernel(window, blocks, places, first_part, last_part, doc_ref, qt_ref, *refs):
    refs = list(refs)
    before = None if first_part else [refs.pop(0) for _ in range(3)]
    kv_refs = refs[:-7]
    *out_refs, k_all, vt_all, s_all, p_all = refs[-7:]
    width = qt_ref.shape[1]
    heads = width // HEAD_SIZE
    first = lax.axis_index("ctx") * blocks
    at = 0
    for ref in kv_refs:
        rows = ref.shape[0]
        k_all[pl.ds(at, rows), :] = ref[:, :HEAD_SIZE]
        vt_all[:, pl.ds(at, rows)] = ref[:, HEAD_SIZE:].T
        at += rows
    for b in range(blocks):
        qt = qt_ref[block(b), :]
        if first_part:
            out, top, total = None, jnp.full((1, width), LOW, jnp.float32), None
        else:
            out, top, total = before[0][block(b), :], *(r[pl.ds(b, 1), :] for r in before[1:])
        earlier = top
        inside = [i for i, place in enumerate(places) if b <= place < b + window]
        start, stop = inside[0], inside[-1] + 1
        ok = {i: allowed(doc_ref, first - (window - 1) + places[i], first + b) for i in inside}
        for i in inside:
            s = dot(k_all[block(i), :], qt) * SCALE2
            if places[i] == b + window - 1:
                s = jnp.where(causal(width), s, LOW)
            s_all[block(i - start), :] = s
            top = jnp.maximum(top, jnp.max(s, axis=0, keepdims=True) + jnp.where(ok[i], 0.0, LOW))
        sums = jnp.zeros((1, width), jnp.float32)
        for i in inside:
            p = jnp.exp2(s_all[block(i - start), :] - jnp.where(ok[i], top, HIGH))
            sums += jnp.sum(p, axis=0, keepdims=True)
            p_all[block(i - start), :] = p.astype(jnp.bfloat16)
        fresh = dot(vt_all[:, block(start, stop - start)], p_all[block(0, stop - start), :])
        if first_part:
            out, total = fresh, sums
        else:
            factor = jnp.exp2(earlier - top)
            out, total = out * factor + fresh, total * factor + sums
        if last_part:
            attn_ref, ot_ref, lse_ref = out_refs
            out = out / total
            ot_ref[block(b), :] = out.astype(jnp.bfloat16)
            lse_ref[pl.ds(b, 1), :] = top + jnp.log2(total)
            for h in range(heads):
                attn_ref[block(b), block(h)] = out[:, h * BLK:(h + 1) * BLK].T.astype(jnp.bfloat16)
        else:
            out_ref, top_ref, total_ref = out_refs
            out_ref[block(b), :] = out
            top_ref[pl.ds(b, 1), :] = top
            total_ref[pl.ds(b, 1), :] = total


def forward(doc_ids, qt, before, kvs, places, window, last_part, cost):
    rows, width = qt.shape
    blocks = rows // BLK
    held = len(places) * BLK
    used = min(held, window * BLK)
    extra = [] if before is None else list(before)
    stats = jax.ShapeDtypeStruct((blocks, width), jnp.float32)
    if last_part:
        out_shape = [jax.ShapeDtypeStruct((rows, width), jnp.bfloat16)] * 2 + [stats]
    else:
        out_shape = [jax.ShapeDtypeStruct((rows, width), jnp.float32), stats, stats]
    return pl.pallas_call(
        functools.partial(forward_kernel, window, blocks, places, before is None, last_part),
        out_shape=out_shape,
        in_specs=[SMEM] + [VMEM] * (1 + len(extra) + len(kvs)),
        out_specs=[VMEM] * 3,
        scratch_shapes=[
            pltpu.VMEM((held, HEAD_SIZE), jnp.bfloat16),
            pltpu.VMEM((HEAD_SIZE, held), jnp.bfloat16),
            pltpu.VMEM((used, width), jnp.float32),
            pltpu.VMEM((used, width), jnp.bfloat16),
        ],
        compiler_params=pltpu.CompilerParams(vmem_limit_bytes=VMEM_LIMIT),
        cost_estimate=cost,
        name="forward",
    )(doc_ids, qt, *extra, *kvs)


def backward_kernel(
    window, blocks, places, first_part, last_part, taking,
    doc_ref, qt_ref, q_rows_ref, ot_ref, lse_ref, g_ref, *refs
):
    refs = list(refs)
    before_ref = None if first_part else refs.pop(0)
    taken_ref = None if taking is None else refs.pop(0)
    n = (len(refs) - 9) // 2
    kv_refs, dq_ref, dkv_refs = refs[:n], refs[n], refs[n + 1:2 * n + 1]
    k_all, kt_all, v_all, g_rows, gt, p_all, ds_all, dkv_all = refs[2 * n + 1:]
    width = qt_ref.shape[1]
    heads = width // HEAD_SIZE
    me = lax.axis_index("ctx")
    first = me * blocks
    at = 0
    for ref in kv_refs:
        rows = ref.shape[0]
        k_all[pl.ds(at, rows), :] = ref[:, :HEAD_SIZE]
        kt_all[:, pl.ds(at, rows)] = ref[:, :HEAD_SIZE].T
        v_all[pl.ds(at, rows), :] = ref[:, HEAD_SIZE:]
        at += rows
    dkv_all[...] = jnp.zeros_like(dkv_all)
    for b in range(blocks):
        for h in range(heads):
            g = g_ref[block(b), block(h)]
            g_rows[block(h), :] = g
            gt[:, block(h)] = g.T
        qt = qt_ref[block(b), :]
        delta = jnp.sum(
            gt[...].astype(jnp.float32) * ot_ref[block(b), :].astype(jnp.float32),
            axis=0, keepdims=True,
        )
        lse = lse_ref[pl.ds(b, 1), :]
        inside = [i for i, place in enumerate(places) if b <= place < b + window]
        if not inside:
            if first_part:
                dq_ref[block(b), :] = jnp.zeros((BLK, width), jnp.float32)
            else:
                dq_ref[block(b), :] = before_ref[block(b), :]
            continue
        start, stop = inside[0], inside[-1] + 1
        for i in inside:
            ok = allowed(doc_ref, first - (window - 1) + places[i], first + b)
            s = dot(k_all[block(i), :], qt) * SCALE2
            if places[i] == b + window - 1:
                s = jnp.where(causal(width), s, LOW)
            p = jnp.exp2(s - jnp.where(ok, lse, HIGH))
            p_all[block(i - start), :] = p.astype(jnp.bfloat16)
            dp = dot(v_all[block(i), :], gt[...])
            ds_all[block(i - start), :] = (p * (dp - delta)).astype(jnp.bfloat16)
        mine, used = block(start, stop - start), block(0, stop - start)
        q_rows = q_rows_ref[pl.ds(b * width, width), :]
        dkv_all[mine, :HEAD_SIZE] += dot(ds_all[used, :], q_rows) * SCALE
        dkv_all[mine, HEAD_SIZE:] += dot(p_all[used, :], g_rows[...])
        dqt = dot(kt_all[:, mine], ds_all[used, :]) * SCALE
        if not first_part:
            dqt += before_ref[block(b), :]
        if last_part:
            for h in range(heads):
                dq_ref[block(b), block(h)] = dqt[:, h * BLK:(h + 1) * BLK].T.astype(jnp.bfloat16)
        else:
            dq_ref[block(b), :] = dqt
    at = 0
    for ref in dkv_refs:
        rows = ref.shape[0]
        total = dkv_all[pl.ds(at, rows), :]
        at += rows
        if taken_ref is not None and ref is dkv_refs[-1]:
            total += jnp.where(me % 2 == taking, taken_ref[...].astype(jnp.float32), 0.0)
        ref[...] = total.astype(ref.dtype)


def backward(doc_ids, qt, q_rows, ot, lse, g, before, taken, kvs, places, window, last_part):
    rows, width = qt.shape
    blocks = rows // BLK
    held = len(places) * BLK
    used = min(held, window * BLK)
    extra = [] if before is None else [before]
    extra += [] if taken is None else [taken[0]]
    kind = jnp.float32 if last_part else jnp.bfloat16
    dq_kind = jnp.bfloat16 if last_part else jnp.float32
    return pl.pallas_call(
        functools.partial(
            backward_kernel, window, blocks, places, before is None, last_part,
            None if taken is None else taken[1],
        ),
        out_shape=[jax.ShapeDtypeStruct((rows, width), dq_kind)]
        + [jax.ShapeDtypeStruct(kv.shape, kind) for kv in kvs],
        in_specs=[SMEM] + [VMEM] * (5 + len(extra) + len(kvs)),
        out_specs=[VMEM] * (1 + len(kvs)),
        scratch_shapes=[
            pltpu.VMEM((held, HEAD_SIZE), jnp.bfloat16),
            pltpu.VMEM((HEAD_SIZE, held), jnp.bfloat16),
            pltpu.VMEM((held, HEAD_SIZE), jnp.bfloat16),
            pltpu.VMEM((width, HEAD_SIZE), jnp.bfloat16),
            pltpu.VMEM((HEAD_SIZE, width), jnp.bfloat16),
            pltpu.VMEM((used, width), jnp.bfloat16),
            pltpu.VMEM((used, width), jnp.bfloat16),
            pltpu.VMEM((held, 2 * HEAD_SIZE), jnp.float32),
        ],
        compiler_params=pltpu.CompilerParams(vmem_limit_bytes=VMEM_LIMIT),
        cost_estimate=COST,
        name="backward",
    )(doc_ids, qt, q_rows, ot, lse, g, *extra, *kvs)


def part_of(w_ref, which, part):
    me = lax.axis_index("tp") ^ which
    return w_ref[:, pl.ds(pl.multiple_of(me * part, BLK), part)]


def features_in_kernel(which, *refs):
    *cots, w_ref, out_ref = refs
    part = cots[0].shape[1]
    total = None if len(cots) == len(which) else cots[-1][...]
    for j, cot in zip(which, cots):
        product = lax.dot_general(
            cot[...], part_of(w_ref, j, part), (((1,), (1,)), ((), ())),
            preferred_element_type=jnp.float32,
        )
        total = product if total is None else total + product
    out_ref[...] = total.astype(out_ref.dtype)


def features_in(which, cots, weight, base, dtype):
    rows, part = cots[0].shape
    depth = weight.shape[0]
    extra = [] if base is None else [base]
    return pl.pallas_call(
        functools.partial(features_in_kernel, which),
        out_shape=jax.ShapeDtypeStruct((rows, depth), dtype),
        in_specs=[VMEM] * (len(cots) + len(extra) + 1),
        out_specs=VMEM,
        compiler_params=pltpu.CompilerParams(vmem_limit_bytes=VMEM_LIMIT),
        cost_estimate=COST,
        name="features_in",
    )(*cots, *extra, weight)


def features_out_kernel(which, attn_ref, *refs):
    *extra, w_ref, out_ref = refs
    total = dot(attn_ref[...], part_of(w_ref, which, out_ref.shape[1]))
    for ref in extra:
        total = total + ref[...].astype(jnp.float32)
    out_ref[...] = total.astype(out_ref.dtype)


def features_out(which, attn, weight, part, extra=(), dtype=jnp.bfloat16):
    rows, depth = attn.shape
    return pl.pallas_call(
        functools.partial(features_out_kernel, which),
        out_shape=jax.ShapeDtypeStruct((rows, part), dtype),
        in_specs=[VMEM] * (2 + len(extra)),
        out_specs=VMEM,
        compiler_params=pltpu.CompilerParams(vmem_limit_bytes=VMEM_LIMIT),
        cost_estimate=COST,
        name="features_out",
    )(attn, *extra, weight)


def join_kernel(k_hbm, v_hbm, whole_ref, last_ref, k, v, sems):
    copies = [
        pltpu.make_async_copy(k_hbm, k, sems.at[0]),
        pltpu.make_async_copy(v_hbm, v, sems.at[1]),
    ]
    for copy in copies:
        copy.start()
    for copy in copies:
        copy.wait()
    skipped = k.shape[0] - last_ref.shape[0]
    whole_ref[:, :HEAD_SIZE] = k[...]
    whole_ref[:, HEAD_SIZE:] = v[...]
    last_ref[:, :HEAD_SIZE] = k[skipped:, :]
    last_ref[:, HEAD_SIZE:] = v[skipped:, :]


def join(keys, values, last):
    rows, width = keys.shape
    return pl.pallas_call(
        join_kernel,
        out_shape=[jax.ShapeDtypeStruct((n, 2 * width), keys.dtype) for n in (rows, last)],
        in_specs=[HBM] * 2,
        out_specs=[VMEM] * 2,
        scratch_shapes=[pltpu.VMEM(keys.shape, keys.dtype)] * 2 + [pltpu.SemaphoreType.DMA((2,))],
        compiler_params=pltpu.CompilerParams(vmem_limit_bytes=VMEM_LIMIT),
        cost_estimate=COST,
        name="join",
    )(in_hbm(keys), in_hbm(values))


def prepare_kernel(
    q_hbm, cot_hbm, cot_c_ref, w_hbm, near_ref, w_ref, qt_ref, q_rows_ref, q_ref, cot_ref, sems
):
    part = cot_ref.shape[1]
    rows, width = q_ref.shape
    me = lax.axis_index("tp")
    pairs = [(q_hbm, q_ref), (cot_hbm, cot_ref)]
    for j in range(4):
        columns = pl.ds(pl.multiple_of((me ^ j) * part, BLK), part)
        pairs.append((w_hbm.at[:, columns], w_ref.at[:, columns]))
    copies = [pltpu.make_async_copy(*pair, sems.at[i]) for i, pair in enumerate(pairs)]
    for copy in copies:
        copy.start()
    copies[0].wait()
    for b in range(rows // BLK):
        for h in range(width // BLK):
            q = q_ref[block(b), block(h)]
            qt_ref[block(b), block(h)] = q.T
            q_rows_ref[pl.ds(b * width + h * BLK, BLK), :] = q
    copies[1].wait()
    for j, cot in ((0, cot_ref), (1, cot_c_ref)):
        copies[2 + j].wait()
        product = lax.dot_general(
            cot[...], part_of(w_ref, j, part), (((1,), (1,)), ((), ())),
            preferred_element_type=jnp.float32,
        )
        near_ref[...] = product if j == 0 else near_ref[...] + product
    copies[4].wait()
    copies[5].wait()


def prepare(q, cot, cot_c, weight):
    rows, width = q.shape
    blocks = rows // BLK
    return pl.pallas_call(
        prepare_kernel,
        out_shape=[
            jax.ShapeDtypeStruct((rows, width), jnp.float32),
            jax.ShapeDtypeStruct(weight.shape, weight.dtype),
            jax.ShapeDtypeStruct((rows, width), q.dtype),
            jax.ShapeDtypeStruct((blocks * width, BLK), q.dtype),
        ],
        in_specs=[HBM, HBM, VMEM, HBM],
        out_specs=[VMEM] * 4,
        scratch_shapes=[
            pltpu.VMEM(q.shape, q.dtype),
            pltpu.VMEM(cot.shape, cot.dtype),
            pltpu.SemaphoreType.DMA((6,)),
        ],
        compiler_params=pltpu.CompilerParams(vmem_limit_bytes=VMEM_LIMIT),
        cost_estimate=COST,
        name="prepare",
    )(in_hbm(q), in_hbm(cot), cot_c, in_hbm(weight))


def on_device(queries, keys, values, out_weight, cotangent, doc_ids):
    rows = queries.shape[0]
    part = cotangent.shape[1]
    ctx_count = lax.axis_size("ctx")
    blocks = rows // BLK
    window = min(8 * blocks, blocks * ctx_count // 2)
    needs = []
    left = window - 1
    while left > 0:
        needs.append(min(left, blocks))
        left -= needs[-1]
    odd = lax.axis_index("ctx") % 2
    key_value, tail = join(keys, values, needs[-1] * BLK)
    key_value, tail, cot = lax.optimization_barrier((key_value, tail, cotangent))
    cot_y = swap(cot, 2)
    held = [key_value, None]
    held += [
        shift(tail if n < blocks else key_value, "ctx", s)
        for s, n in enumerate(needs[1:], start=2)
    ]
    held[1] = swap(jnp.where(odd == 0, key_value, held[2]), 1, "ctx")
    near, weight, qt, q_rows = prepare(queries, cot, swap(cot, 1), out_weight)
    def places_of(shards):
        places = []
        for s in shards:
            top = window - 1 - (s - 1) * blocks if s > 0 else window - 1 + blocks
            places += range(top - (needs[s - 1] if s > 0 else blocks), top)
        return tuple(places)

    def part_back(shards, before, taken, last_part):
        return backward(
            doc_ids, qt, q_rows, ot, lse, grad_attn, before, taken,
            [held[s] for s in shards], places_of(shards), window, last_part,
        )

    shards = list(range(len(needs), 1, -1)) + [0]
    state = forward(
        doc_ids, qt, None, [held[s] for s in shards], places_of(shards), window, False, LONG
    )
    attn, ot, lse = forward(doc_ids, qt, state, [held[1]], places_of([1]), window, True, COST)
    attn, cot_y = lax.optimization_barrier((attn, cot_y))
    cot_d = swap(cot_y, 1)
    grad_attn = features_in((2, 3), [cot_y, cot_d], weight, near, jnp.bfloat16)
    out_a = features_out(3, attn, weight, part)

    odds, evens = [list(range(len(needs), 0, -1))[(len(needs) - 1 - i) % 2::2] for i in (0, 1)]
    dq, *odd_parts = part_back(odds, None, None, False)
    taken = swap(odd_parts[-1], 1, "ctx")
    dq, out_a = lax.optimization_barrier((dq, swap(out_a, 1)))
    out_b = features_out(2, attn, weight, part, [out_a])
    from_y = swap(out_b, 2)
    dq, *even_parts = part_back(evens, dq, (taken, 1), False)
    dq, own = part_back([0], dq, (taken, 0), True)
    parts = dict(zip(odds, odd_parts)) | dict(zip(evens, even_parts))
    backs = {s: shift(parts[s], "ctx", -s) for s in range(2, len(held))}
    out_c = features_out(1, attn, weight, part)
    out_d = features_out(0, attn, weight, part, [swap(out_c, 1)], jnp.float32)
    backs, out_d = lax.optimization_barrier((backs, out_d))
    for s, back in backs.items():
        back = back.astype(jnp.float32)
        own = own + jnp.pad(back, ((rows - back.shape[0], 0), (0, 0)))
    mixed = (out_d + from_y.astype(jnp.float32)).astype(jnp.bfloat16)
    return (
        mixed,
        dq,
        own[:, :HEAD_SIZE].astype(jnp.bfloat16),
        own[:, HEAD_SIZE:].astype(jnp.bfloat16),
    )


def solution(mesh):
    return jax.shard_map(
        on_device,
        mesh=mesh,
        in_specs=(
            P("ctx", "tp"),
            P("ctx", "tp"),
            P("ctx", "tp"),
            P("tp", None),
            P("ctx", "tp"),
            P(),
        ),
        out_specs=(P("ctx", "tp"), P("ctx", "tp"), P("ctx", "tp"), P("ctx", "tp")),
        check_vma=False,
    )
```

```python
import functools
import math

import jax
import jax.numpy as jnp
from jax import lax
from jax.experimental import pallas as pl
from jax.experimental.pallas import tpu as pltpu
from jax.sharding import PartitionSpec as P

HEAD_SIZE = 128
BLK = 128
SCALE = 1.0 / math.sqrt(HEAD_SIZE)
SCALE2 = SCALE * math.log2(math.e)
LOW = -1e30
HIGH = 1e30
VMEM_LIMIT = 16 * 1024 * 1024

COST = pl.CostEstimate(flops=2**20, bytes_accessed=2**10, transcendentals=0)
LONG = pl.CostEstimate(flops=2**31, bytes_accessed=2**10, transcendentals=0)

SHORT = pl.CostEstimate(flops=1073741824, bytes_accessed=2**10, transcendentals=0)
HBM = pl.BlockSpec(memory_space=pltpu.HBM)
VMEM = pl.BlockSpec(memory_space=pltpu.VMEM)
SMEM = pl.BlockSpec(memory_space=pltpu.SMEM)


def in_hbm(array):
    return pltpu.with_memory_space_constraint(array, pltpu.HBM)


def dot(a, b):
    return jnp.dot(a, b, preferred_element_type=jnp.float32)


def shift(array, axis, by):
    devices = lax.axis_size(axis)
    pairs = [(i, i + by) for i in range(devices) if 0 <= i + by < devices]
    return lax.ppermute(array, axis, pairs)


def turn(array, axis, by):
    devices = lax.axis_size(axis)
    return lax.ppermute(array, axis, [(i, (i + by) % devices) for i in range(devices)])


def swap(array, bit, axis="tp"):
    return lax.ppermute(array, axis, [(i, i ^ bit) for i in range(lax.axis_size(axis))])


def block(i, n=1):
    return pl.ds(i * BLK, n * BLK)


def allowed(doc_ref, key_block, query_block):
    return (key_block >= 0) & (doc_ref[jnp.maximum(key_block, 0)] == doc_ref[query_block])


def causal(width):
    key = lax.broadcasted_iota(jnp.int32, (BLK, width), 0)
    query = lax.broadcasted_iota(jnp.int32, (BLK, width), 1) % BLK
    return key <= query


def forward_kernel(window, blocks, places, first_part, last_part, doc_ref, qt_ref, *refs):
    refs = list(refs)
    before = None if first_part else [refs.pop(0) for _ in range(3)]
    kv_refs = refs[:-7]
    *out_refs, k_all, vt_all, s_all, p_all = refs[-7:]
    width = qt_ref.shape[1]
    heads = width // HEAD_SIZE
    first = lax.axis_index("ctx") * blocks
    at = 0
    for ref in kv_refs:
        rows = ref.shape[0]
        k_all[pl.ds(at, rows), :] = ref[:, :HEAD_SIZE]
        vt_all[:, pl.ds(at, rows)] = ref[:, HEAD_SIZE:].T
        at += rows
    for b in range(blocks):
        qt = qt_ref[block(b), :]
        if first_part:
            out, top, total = None, jnp.full((1, width), LOW, jnp.float32), None
        else:
            out, top, total = before[0][block(b), :], *(r[pl.ds(b, 1), :] for r in before[1:])
        earlier = top
        inside = [i for i, place in enumerate(places) if b <= place < b + window]
        start, stop = inside[0], inside[-1] + 1
        ok = {i: allowed(doc_ref, first - (window - 1) + places[i], first + b) for i in inside}
        for i in inside:
            s = dot(k_all[block(i), :], qt) * SCALE2
            if places[i] == b + window - 1:
                s = jnp.where(causal(width), s, LOW)
            s_all[block(i - start), :] = s
            top = jnp.maximum(top, jnp.max(s, axis=0, keepdims=True) + jnp.where(ok[i], 0.0, LOW))
        sums = jnp.zeros((1, width), jnp.float32)
        for i in inside:
            p = jnp.exp2(s_all[block(i - start), :] - jnp.where(ok[i], top, HIGH))
            sums += jnp.sum(p, axis=0, keepdims=True)
            p_all[block(i - start), :] = p.astype(jnp.bfloat16)
        fresh = dot(vt_all[:, block(start, stop - start)], p_all[block(0, stop - start), :])
        if first_part:
            out, total = fresh, sums
        else:
            factor = jnp.exp2(earlier - top)
            out, total = out * factor + fresh, total * factor + sums
        if last_part:
            attn_ref, ot_ref, lse_ref = out_refs
            out = out / total
            ot_ref[block(b), :] = out.astype(jnp.bfloat16)
            lse_ref[pl.ds(b, 1), :] = top + jnp.log2(total)
            for h in range(heads):
                attn_ref[block(b), block(h)] = out[:, h * BLK:(h + 1) * BLK].T.astype(jnp.bfloat16)
        else:
            out_ref, top_ref, total_ref = out_refs
            out_ref[block(b), :] = out
            top_ref[pl.ds(b, 1), :] = top
            total_ref[pl.ds(b, 1), :] = total


def forward(doc_ids, qt, before, kvs, places, window, last_part, cost):
    rows, width = qt.shape
    blocks = rows // BLK
    held = len(places) * BLK
    used = min(held, window * BLK)
    extra = [] if before is None else list(before)
    stats = jax.ShapeDtypeStruct((blocks, width), jnp.float32)
    if last_part:
        out_shape = [jax.ShapeDtypeStruct((rows, width), jnp.bfloat16)] * 2 + [stats]
    else:
        out_shape = [jax.ShapeDtypeStruct((rows, width), jnp.float32), stats, stats]
    return pl.pallas_call(
        functools.partial(forward_kernel, window, blocks, places, before is None, last_part),
        out_shape=out_shape,
        in_specs=[SMEM] + [VMEM] * (1 + len(extra) + len(kvs)),
        out_specs=[VMEM] * 3,
        scratch_shapes=[
            pltpu.VMEM((held, HEAD_SIZE), jnp.bfloat16),
            pltpu.VMEM((HEAD_SIZE, held), jnp.bfloat16),
            pltpu.VMEM((used, width), jnp.float32),
            pltpu.VMEM((used, width), jnp.bfloat16),
        ],
        compiler_params=pltpu.CompilerParams(vmem_limit_bytes=VMEM_LIMIT),
        cost_estimate=cost,
        name="forward",
    )(doc_ids, qt, *extra, *kvs)


def backward_kernel(
    window, blocks, places, first_part, last_part, taking,
    doc_ref, qt_ref, q_rows_ref, ot_ref, lse_ref, g_ref, *refs
):
    refs = list(refs)
    before_ref = None if first_part else refs.pop(0)
    taken_ref = None if taking is None else refs.pop(0)
    n = (len(refs) - 9) // 2
    kv_refs, dq_ref, dkv_refs = refs[:n], refs[n], refs[n + 1:2 * n + 1]
    k_all, kt_all, v_all, g_rows, gt, p_all, ds_all, dkv_all = refs[2 * n + 1:]
    width = qt_ref.shape[1]
    heads = width // HEAD_SIZE
    me = lax.axis_index("ctx")
    first = me * blocks
    at = 0
    for ref in kv_refs:
        rows = ref.shape[0]
        k_all[pl.ds(at, rows), :] = ref[:, :HEAD_SIZE]
        kt_all[:, pl.ds(at, rows)] = ref[:, :HEAD_SIZE].T
        v_all[pl.ds(at, rows), :] = ref[:, HEAD_SIZE:]
        at += rows
    dkv_all[...] = jnp.zeros_like(dkv_all)
    for b in range(blocks):
        for h in range(heads):
            g = g_ref[block(b), block(h)]
            g_rows[block(h), :] = g
            gt[:, block(h)] = g.T
        qt = qt_ref[block(b), :]
        delta = jnp.sum(
            gt[...].astype(jnp.float32) * ot_ref[block(b), :].astype(jnp.float32),
            axis=0, keepdims=True,
        )
        lse = lse_ref[pl.ds(b, 1), :]
        inside = [i for i, place in enumerate(places) if b <= place < b + window]
        if not inside:
            if first_part:
                dq_ref[block(b), :] = jnp.zeros((BLK, width), jnp.float32)
            else:
                dq_ref[block(b), :] = before_ref[block(b), :]
            continue
        start, stop = inside[0], inside[-1] + 1
        for i in inside:
            ok = allowed(doc_ref, first - (window - 1) + places[i], first + b)
            s = dot(k_all[block(i), :], qt) * SCALE2
            if places[i] == b + window - 1:
                s = jnp.where(causal(width), s, LOW)
            p = jnp.exp2(s - jnp.where(ok, lse, HIGH))
            p_all[block(i - start), :] = p.astype(jnp.bfloat16)
            dp = dot(v_all[block(i), :], gt[...])
            ds_all[block(i - start), :] = (p * (dp - delta)).astype(jnp.bfloat16)
        mine, used = block(start, stop - start), block(0, stop - start)
        q_rows = q_rows_ref[pl.ds(b * width, width), :]
        dkv_all[mine, :HEAD_SIZE] += dot(ds_all[used, :], q_rows) * SCALE
        dkv_all[mine, HEAD_SIZE:] += dot(p_all[used, :], g_rows[...])
        dqt = dot(kt_all[:, mine], ds_all[used, :]) * SCALE
        if not first_part:
            dqt += before_ref[block(b), :]
        if last_part:
            for h in range(heads):
                dq_ref[block(b), block(h)] = dqt[:, h * BLK:(h + 1) * BLK].T.astype(jnp.bfloat16)
        else:
            dq_ref[block(b), :] = dqt
    at = 0
    for ref in dkv_refs:
        rows = ref.shape[0]
        total = dkv_all[pl.ds(at, rows), :]
        at += rows
        if taken_ref is not None and ref is dkv_refs[-1]:
            total += jnp.where(me % 2 == taking, taken_ref[...].astype(jnp.float32), 0.0)
        ref[...] = total.astype(ref.dtype)


def backward(doc_ids, qt, q_rows, ot, lse, g, before, taken, kvs, kind, places, window, last_part):
    rows, width = qt.shape
    blocks = rows // BLK
    held = len(places) * BLK
    used = min(held, window * BLK)
    extra = [] if before is None else [before]
    extra += [] if taken is None else [taken[0]]
    dq_kind = jnp.bfloat16 if last_part else jnp.float32
    return pl.pallas_call(
        functools.partial(
            backward_kernel, window, blocks, places, before is None, last_part,
            None if taken is None else taken[1],
        ),
        out_shape=[jax.ShapeDtypeStruct((rows, width), dq_kind)]
        + [jax.ShapeDtypeStruct(kv.shape, kind) for kv in kvs],
        in_specs=[SMEM] + [VMEM] * (5 + len(extra) + len(kvs)),
        out_specs=[VMEM] * (1 + len(kvs)),
        scratch_shapes=[
            pltpu.VMEM((held, HEAD_SIZE), jnp.bfloat16),
            pltpu.VMEM((HEAD_SIZE, held), jnp.bfloat16),
            pltpu.VMEM((held, HEAD_SIZE), jnp.bfloat16),
            pltpu.VMEM((width, HEAD_SIZE), jnp.bfloat16),
            pltpu.VMEM((HEAD_SIZE, width), jnp.bfloat16),
            pltpu.VMEM((used, width), jnp.bfloat16),
            pltpu.VMEM((used, width), jnp.bfloat16),
            pltpu.VMEM((held, 2 * HEAD_SIZE), jnp.float32),
        ],
        compiler_params=pltpu.CompilerParams(vmem_limit_bytes=VMEM_LIMIT),
        cost_estimate=COST,
        name="backward",
    )(doc_ids, qt, q_rows, ot, lse, g, *extra, *kvs)


def part_of(w_ref, which, part):
    me = lax.axis_index("tp") ^ which
    return w_ref[:, pl.ds(pl.multiple_of(me * part, BLK), part)]


def features_in_kernel(which, *refs):
    *cots, w_ref, out_ref = refs
    part = cots[0].shape[1]
    total = None if len(cots) == len(which) else cots[-1][...]
    for j, cot in zip(which, cots):
        product = lax.dot_general(
            cot[...], part_of(w_ref, j, part), (((1,), (1,)), ((), ())),
            preferred_element_type=jnp.float32,
        )
        total = product if total is None else total + product
    out_ref[...] = total.astype(out_ref.dtype)


def features_in(which, cots, weight, base, dtype):
    rows, part = cots[0].shape
    depth = weight.shape[0]
    extra = [] if base is None else [base]
    return pl.pallas_call(
        functools.partial(features_in_kernel, which),
        out_shape=jax.ShapeDtypeStruct((rows, depth), dtype),
        in_specs=[VMEM] * (len(cots) + len(extra) + 1),
        out_specs=VMEM,
        compiler_params=pltpu.CompilerParams(vmem_limit_bytes=VMEM_LIMIT),
        cost_estimate=COST,
        name="features_in",
    )(*cots, *extra, weight)


def features_out_kernel(which, attn_ref, *refs):
    *extra, w_ref, out_ref = refs
    total = dot(attn_ref[...], part_of(w_ref, which, out_ref.shape[1]))
    for ref in extra:
        total = total + ref[...].astype(jnp.float32)
    out_ref[...] = total.astype(out_ref.dtype)


def features_out(which, attn, weight, part, extra=(), dtype=jnp.bfloat16):
    rows, depth = attn.shape
    return pl.pallas_call(
        functools.partial(features_out_kernel, which),
        out_shape=jax.ShapeDtypeStruct((rows, part), dtype),
        in_specs=[VMEM] * (2 + len(extra)),
        out_specs=VMEM,
        compiler_params=pltpu.CompilerParams(vmem_limit_bytes=VMEM_LIMIT),
        cost_estimate=COST,
        name="features_out",
    )(attn, *extra, weight)


def join_kernel(k_hbm, v_hbm, whole_ref, last_ref, k, v, sems):
    copies = [
        pltpu.make_async_copy(k_hbm, k, sems.at[0]),
        pltpu.make_async_copy(v_hbm, v, sems.at[1]),
    ]
    for copy in copies:
        copy.start()
    for copy in copies:
        copy.wait()
    skipped = k.shape[0] - last_ref.shape[0]
    whole_ref[:, :HEAD_SIZE] = k[...]
    whole_ref[:, HEAD_SIZE:] = v[...]
    last_ref[:, :HEAD_SIZE] = k[skipped:, :]
    last_ref[:, HEAD_SIZE:] = v[skipped:, :]


def join(keys, values, last):
    rows, width = keys.shape
    return pl.pallas_call(
        join_kernel,
        out_shape=[jax.ShapeDtypeStruct((n, 2 * width), keys.dtype) for n in (rows, last)],
        in_specs=[HBM] * 2,
        out_specs=[VMEM] * 2,
        scratch_shapes=[pltpu.VMEM(keys.shape, keys.dtype)] * 2 + [pltpu.SemaphoreType.DMA((2,))],
        compiler_params=pltpu.CompilerParams(vmem_limit_bytes=VMEM_LIMIT),
        cost_estimate=COST,
        name="join",
    )(in_hbm(keys), in_hbm(values))


def prepare_kernel(
    q_hbm, cot_hbm, cot_c_ref, w_hbm, near_ref, w_ref, qt_ref, q_rows_ref, q_ref, cot_ref, sems
):
    part = cot_ref.shape[1]
    rows, width = q_ref.shape
    me = lax.axis_index("tp")
    pairs = [(q_hbm, q_ref), (cot_hbm, cot_ref)]
    for j in range(4):
        columns = pl.ds(pl.multiple_of((me ^ j) * part, BLK), part)
        pairs.append((w_hbm.at[:, columns], w_ref.at[:, columns]))
    copies = [pltpu.make_async_copy(*pair, sems.at[i]) for i, pair in enumerate(pairs)]
    for copy in copies:
        copy.start()
    copies[0].wait()
    for b in range(rows // BLK):
        for h in range(width // BLK):
            q = q_ref[block(b), block(h)]
            qt_ref[block(b), block(h)] = q.T
            q_rows_ref[pl.ds(b * width + h * BLK, BLK), :] = q
    copies[1].wait()
    for j, cot in ((0, cot_ref), (1, cot_c_ref)):
        copies[2 + j].wait()
        product = lax.dot_general(
            cot[...], part_of(w_ref, j, part), (((1,), (1,)), ((), ())),
            preferred_element_type=jnp.float32,
        )
        near_ref[...] = product if j == 0 else near_ref[...] + product
    copies[4].wait()
    copies[5].wait()


def prepare(q, cot, cot_c, weight):
    rows, width = q.shape
    blocks = rows // BLK
    return pl.pallas_call(
        prepare_kernel,
        out_shape=[
            jax.ShapeDtypeStruct((rows, width), jnp.float32),
            jax.ShapeDtypeStruct(weight.shape, weight.dtype),
            jax.ShapeDtypeStruct((rows, width), q.dtype),
            jax.ShapeDtypeStruct((blocks * width, BLK), q.dtype),
        ],
        in_specs=[HBM, HBM, VMEM, HBM],
        out_specs=[VMEM] * 4,
        scratch_shapes=[
            pltpu.VMEM(q.shape, q.dtype),
            pltpu.VMEM(cot.shape, cot.dtype),
            pltpu.SemaphoreType.DMA((6,)),
        ],
        compiler_params=pltpu.CompilerParams(vmem_limit_bytes=VMEM_LIMIT),
        cost_estimate=COST,
        name="prepare",
    )(in_hbm(q), in_hbm(cot), cot_c, in_hbm(weight))


def add_kernel(*refs):
    *in_refs, out_ref = refs
    rows = out_ref.shape[0]
    out_ref[...] = in_refs[0][...]
    for ref in in_refs[1:]:
        count = ref.shape[0]
        out_ref[pl.ds(rows - count, count), :] += ref[...].astype(jnp.float32)


def add_up(arrays, cost):
    return pl.pallas_call(
        add_kernel,
        out_shape=jax.ShapeDtypeStruct(arrays[0].shape, jnp.float32),
        in_specs=[VMEM] * len(arrays),
        out_specs=VMEM,
        compiler_params=pltpu.CompilerParams(vmem_limit_bytes=VMEM_LIMIT),
        cost_estimate=cost,
        name="add_up",
    )(*arrays)


def finish_kernel(out_ref, other_ref, own_ref, back_ref, mixed_hbm, dk_hbm, dv_hbm,
                  mixed, dk, dv, sems):
    half = mixed.shape[0] // 2
    copies = [pltpu.make_async_copy(dk, dk_hbm, sems.at[0])]
    copies.append(pltpu.make_async_copy(dv, dv_hbm, sems.at[1]))
    total = own_ref[...] + back_ref[...].astype(jnp.float32)
    dk[...] = total[:, :HEAD_SIZE].astype(dk.dtype)
    dv[...] = total[:, HEAD_SIZE:].astype(dv.dtype)
    copies[0].start()
    copies[1].start()
    for i in range(2):
        rows = pl.ds(i * half, half)
        mixed[rows, :] = (out_ref[rows, :] + other_ref[rows, :].astype(jnp.float32)).astype(
            mixed.dtype
        )
        copies.append(
            pltpu.make_async_copy(mixed.at[rows, :], mixed_hbm.at[rows, :], sems.at[2 + i])
        )
        copies[-1].start()
    for copy in copies:
        copy.wait()


def finish(out, other, own, back):
    rows = own.shape[0]
    kinds = [
        jax.ShapeDtypeStruct(out.shape, jnp.bfloat16),
        jax.ShapeDtypeStruct((rows, HEAD_SIZE), jnp.bfloat16),
        jax.ShapeDtypeStruct((rows, HEAD_SIZE), jnp.bfloat16),
    ]
    return pl.pallas_call(
        finish_kernel,
        out_shape=kinds,
        in_specs=[VMEM] * 4,
        out_specs=[HBM] * 3,
        scratch_shapes=[pltpu.VMEM(kind.shape, kind.dtype) for kind in kinds]
        + [pltpu.SemaphoreType.DMA((4,))],
        compiler_params=pltpu.CompilerParams(vmem_limit_bytes=VMEM_LIMIT),
        cost_estimate=COST,
        name="finish",
    )(out, other, own, back)


def on_device(queries, keys, values, out_weight, cotangent, doc_ids):
    rows = queries.shape[0]
    part = cotangent.shape[1]
    ctx_count = lax.axis_size("ctx")
    blocks = rows // BLK
    window = min(8 * blocks, blocks * ctx_count // 2)
    needs = []
    left = window - 1
    while left > 0:
        needs.append(min(left, blocks))
        left -= needs[-1]
    odd = lax.axis_index("ctx") % 2
    key_value, tail = join(keys, values, needs[-1] * BLK)
    key_value, tail, cot = lax.optimization_barrier((key_value, tail, cotangent))
    cot_y = swap(cot, 2)
    held = [key_value, None]
    held += [
        (shift if s % 2 else turn)(tail if n < blocks else key_value, "ctx", s)
        for s, n in enumerate(needs[1:], start=2)
    ]
    held[1] = swap(jnp.where(odd == 0, key_value, held[2]), 1, "ctx")
    near, weight, qt, q_rows = prepare(queries, cot, swap(cot, 1), out_weight)
    def places_of(shards):
        places = []
        for s in shards:
            top = window - 1 - (s - 1) * blocks if s > 0 else window - 1 + blocks
            places += range(top - (needs[s - 1] if s > 0 else blocks), top)
        return tuple(places)

    def part_back(shards, before, taken, last_part):
        return backward(
            doc_ids, qt, q_rows, ot, lse, grad_attn, before, taken,
            [held[s] for s in shards], jnp.bfloat16 if shards[0] else jnp.float32,
            places_of(shards), window, last_part,
        )

    shards = list(range(len(needs), 1, -1)) + [0]
    state = forward(
        doc_ids, qt, None, [held[s] for s in shards], places_of(shards), window, False, LONG
    )
    attn, ot, lse = forward(doc_ids, qt, state, [held[1]], places_of([1]), window, True, COST)
    attn, cot_y = lax.optimization_barrier((attn, cot_y))
    cot_d = swap(cot_y, 1)
    grad_attn = features_in((2, 3), [cot_y, cot_d], weight, near, jnp.bfloat16)
    out_a = features_out(3, attn, weight, part)

    out_b = features_out(2, attn, weight, part, [swap(out_a, 1)])
    from_y = swap(out_b, 2)
    most = list(range(len(needs), 2, -1))
    dq, *parts = part_back(most + [1], None, None, False)
    taken = swap(parts[-1], 1, "ctx")
    parts = dict(zip(most, parts))
    dq, parts[2] = part_back([2], dq, (taken, 1), False)
    dq, own = part_back([0], dq, (taken, 0), True)
    backs = {s: turn(parts[s], "ctx", -s) for s in range(2, len(held))}
    out_c = features_out(1, attn, weight, part)
    out_d = features_out(0, attn, weight, part, [swap(out_c, 1)], jnp.float32)
    own = add_up([own] + [backs[s] for s in most], SHORT)
    mixed, dk, dv = finish(out_d, from_y, own, backs[2])
    return (mixed, dq, dk, dv)


def solution(mesh):
    return jax.shard_map(
        on_device,
        mesh=mesh,
        in_specs=(
            P("ctx", "tp"),
            P("ctx", "tp"),
            P("ctx", "tp"),
            P("tp", None),
            P("ctx", "tp"),
            P(),
        ),
        out_specs=(P("ctx", "tp"), P("ctx", "tp"), P("ctx", "tp"), P("ctx", "tp")),
        check_vma=False,
    )
```

```python
import functools
import math

import jax
import jax.numpy as jnp
from jax import lax
from jax.experimental import pallas as pl
from jax.experimental.pallas import tpu as pltpu
from jax.sharding import PartitionSpec as P

HEAD_SIZE = 128
BLK = 128
SCALE = 1.0 / math.sqrt(HEAD_SIZE)
SCALE2 = SCALE * math.log2(math.e)
LOW = -1e30
HIGH = 1e30
VMEM_LIMIT = 16 * 1024 * 1024

COST = pl.CostEstimate(flops=2**20, bytes_accessed=2**10, transcendentals=0)
LONG = pl.CostEstimate(flops=2**31, bytes_accessed=2**10, transcendentals=0)

SHORT = pl.CostEstimate(flops=1073741824, bytes_accessed=2**10, transcendentals=0)
HBM = pl.BlockSpec(memory_space=pltpu.HBM)
VMEM = pl.BlockSpec(memory_space=pltpu.VMEM)
SMEM = pl.BlockSpec(memory_space=pltpu.SMEM)


def in_hbm(array):
    return pltpu.with_memory_space_constraint(array, pltpu.HBM)


def dot(a, b):
    return jnp.dot(a, b, preferred_element_type=jnp.float32)


def shift(array, axis, by):
    devices = lax.axis_size(axis)
    pairs = [(i, i + by) for i in range(devices) if 0 <= i + by < devices]
    return lax.ppermute(array, axis, pairs)


def turn(array, axis, by):
    devices = lax.axis_size(axis)
    return lax.ppermute(array, axis, [(i, (i + by) % devices) for i in range(devices)])


def swap(array, bit, axis="tp"):
    return lax.ppermute(array, axis, [(i, i ^ bit) for i in range(lax.axis_size(axis))])


def block(i, n=1):
    return pl.ds(i * BLK, n * BLK)


def allowed(doc_ref, key_block, query_block):
    return (key_block >= 0) & (doc_ref[jnp.maximum(key_block, 0)] == doc_ref[query_block])


def causal(width):
    key = lax.broadcasted_iota(jnp.int32, (BLK, width), 0)
    query = lax.broadcasted_iota(jnp.int32, (BLK, width), 1) % BLK
    return key <= query


def forward_kernel(window, blocks, places, first_part, last_part, doc_ref, qt_ref, *refs):
    refs = list(refs)
    before = None if first_part else [refs.pop(0) for _ in range(3)]
    kv_refs = refs[:-7]
    *out_refs, k_all, vt_all, s_all, p_all = refs[-7:]
    width = qt_ref.shape[1]
    heads = width // HEAD_SIZE
    first = lax.axis_index("ctx") * blocks
    at = 0
    for ref in kv_refs:
        rows = ref.shape[0]
        k_all[pl.ds(at, rows), :] = ref[:, :HEAD_SIZE]
        vt_all[:, pl.ds(at, rows)] = ref[:, HEAD_SIZE:].T
        at += rows
    for b in range(blocks):
        qt = qt_ref[block(b), :]
        if first_part:
            out, top, total = None, jnp.full((1, width), LOW, jnp.float32), None
        else:
            out, top, total = before[0][block(b), :], *(r[pl.ds(b, 1), :] for r in before[1:])
        earlier = top
        inside = [i for i, place in enumerate(places) if b <= place < b + window]
        start, stop = inside[0], inside[-1] + 1
        ok = {i: allowed(doc_ref, first - (window - 1) + places[i], first + b) for i in inside}
        for i in inside:
            s = dot(k_all[block(i), :], qt) * SCALE2
            if places[i] == b + window - 1:
                s = jnp.where(causal(width), s, LOW)
            s_all[block(i - start), :] = s
            top = jnp.maximum(top, jnp.max(s, axis=0, keepdims=True) + jnp.where(ok[i], 0.0, LOW))
        sums = jnp.zeros((1, width), jnp.float32)
        for i in inside:
            p = jnp.exp2(s_all[block(i - start), :] - jnp.where(ok[i], top, HIGH))
            sums += jnp.sum(p, axis=0, keepdims=True)
            p_all[block(i - start), :] = p.astype(jnp.bfloat16)
        fresh = dot(vt_all[:, block(start, stop - start)], p_all[block(0, stop - start), :])
        if first_part:
            out, total = fresh, sums
        else:
            factor = jnp.exp2(earlier - top)
            out, total = out * factor + fresh, total * factor + sums
        if last_part:
            attn_ref, ot_ref, lse_ref = out_refs
            out = (out / total).astype(jnp.bfloat16)
            ot_ref[block(b), :] = out
            lse_ref[pl.ds(b, 1), :] = top + jnp.log2(total)
            for h in range(heads):
                attn_ref[block(b), block(h)] = out[:, h * BLK:(h + 1) * BLK].T
        else:
            out_ref, top_ref, total_ref = out_refs
            out_ref[block(b), :] = out
            top_ref[pl.ds(b, 1), :] = top
            total_ref[pl.ds(b, 1), :] = total


def forward(doc_ids, qt, before, kvs, places, window, last_part, cost):
    rows, width = qt.shape
    blocks = rows // BLK
    held = len(places) * BLK
    used = min(held, window * BLK)
    extra = [] if before is None else list(before)
    stats = jax.ShapeDtypeStruct((blocks, width), jnp.float32)
    if last_part:
        out_shape = [jax.ShapeDtypeStruct((rows, width), jnp.bfloat16)] * 2 + [stats]
    else:
        out_shape = [jax.ShapeDtypeStruct((rows, width), jnp.float32), stats, stats]
    return pl.pallas_call(
        functools.partial(forward_kernel, window, blocks, places, before is None, last_part),
        out_shape=out_shape,
        in_specs=[SMEM] + [VMEM] * (1 + len(extra) + len(kvs)),
        out_specs=[VMEM] * 3,
        scratch_shapes=[
            pltpu.VMEM((held, HEAD_SIZE), jnp.bfloat16),
            pltpu.VMEM((HEAD_SIZE, held), jnp.bfloat16),
            pltpu.VMEM((used, width), jnp.float32),
            pltpu.VMEM((used, width), jnp.bfloat16),
        ],
        compiler_params=pltpu.CompilerParams(vmem_limit_bytes=VMEM_LIMIT),
        cost_estimate=cost,
        name="forward",
    )(doc_ids, qt, *extra, *kvs)


def backward_kernel(
    window, blocks, places, first_part, last_part, taking,
    doc_ref, qt_ref, q_rows_ref, lse_ref, gt_ref, g_rows_ref, delta_ref, *refs
):
    refs = list(refs)
    before_ref = None if first_part else refs.pop(0)
    taken_ref = None if taking is None else refs.pop(0)
    n = (len(refs) - 7) // 2
    kv_refs, dq_ref, dkv_refs = refs[:n], refs[n], refs[n + 1:2 * n + 1]
    k_all, kt_all, v_all, p_all, ds_all, dkv_all = refs[2 * n + 1:]
    width = qt_ref.shape[1]
    heads = width // HEAD_SIZE
    me = lax.axis_index("ctx")
    first = me * blocks
    at = 0
    for ref in kv_refs:
        rows = ref.shape[0]
        k_all[pl.ds(at, rows), :] = ref[:, :HEAD_SIZE]
        kt_all[:, pl.ds(at, rows)] = ref[:, :HEAD_SIZE].T
        v_all[pl.ds(at, rows), :] = ref[:, HEAD_SIZE:]
        at += rows
    dkv_all[...] = jnp.zeros_like(dkv_all)
    for b in range(blocks):
        qt, gt = qt_ref[block(b), :], gt_ref[block(b), :]
        delta = delta_ref[pl.ds(b, 1), :]
        lse = lse_ref[pl.ds(b, 1), :]
        inside = [i for i, place in enumerate(places) if b <= place < b + window]
        if not inside:
            if first_part:
                dq_ref[block(b), :] = jnp.zeros((BLK, width), jnp.float32)
            else:
                dq_ref[block(b), :] = before_ref[block(b), :]
            continue
        start, stop = inside[0], inside[-1] + 1
        for i in inside:
            ok = allowed(doc_ref, first - (window - 1) + places[i], first + b)
            s = dot(k_all[block(i), :], qt) * SCALE2
            if places[i] == b + window - 1:
                s = jnp.where(causal(width), s, LOW)
            p = jnp.exp2(s - jnp.where(ok, lse, HIGH))
            p_all[block(i - start), :] = p.astype(jnp.bfloat16)
            dp = dot(v_all[block(i), :], gt)
            ds_all[block(i - start), :] = (p * (dp - delta)).astype(jnp.bfloat16)
        mine, used = block(start, stop - start), block(0, stop - start)
        stacked = pl.ds(b * width, width)
        dkv_all[mine, :HEAD_SIZE] += dot(ds_all[used, :], q_rows_ref[stacked, :]) * SCALE
        dkv_all[mine, HEAD_SIZE:] += dot(p_all[used, :], g_rows_ref[stacked, :])
        dqt = dot(kt_all[:, mine], ds_all[used, :]) * SCALE
        if not first_part:
            dqt += before_ref[block(b), :]
        if last_part:
            dqt = dqt.astype(jnp.bfloat16)
            for h in range(heads):
                dq_ref[block(b), block(h)] = dqt[:, h * BLK:(h + 1) * BLK].T
        else:
            dq_ref[block(b), :] = dqt
    at = 0
    for ref in dkv_refs:
        rows = ref.shape[0]
        total = dkv_all[pl.ds(at, rows), :]
        at += rows
        if taken_ref is not None and ref is dkv_refs[-1]:
            total += jnp.where(me % 2 == taking, taken_ref[...].astype(jnp.float32), 0.0)
        ref[...] = total.astype(ref.dtype)


def backward(doc_ids, qt, q_rows, lse, grads, before, taken, kvs, kind, places, window, last_part):
    rows, width = qt.shape
    blocks = rows // BLK
    held = len(places) * BLK
    used = min(held, window * BLK)
    extra = [] if before is None else [before]
    extra += [] if taken is None else [taken[0]]
    dq_kind = jnp.bfloat16 if last_part else jnp.float32
    return pl.pallas_call(
        functools.partial(
            backward_kernel, window, blocks, places, before is None, last_part,
            None if taken is None else taken[1],
        ),
        out_shape=[jax.ShapeDtypeStruct((rows, width), dq_kind)]
        + [jax.ShapeDtypeStruct(kv.shape, kind) for kv in kvs],
        in_specs=[SMEM] + [VMEM] * (6 + len(extra) + len(kvs)),
        out_specs=[VMEM] * (1 + len(kvs)),
        scratch_shapes=[
            pltpu.VMEM((held, HEAD_SIZE), jnp.bfloat16),
            pltpu.VMEM((HEAD_SIZE, held), jnp.bfloat16),
            pltpu.VMEM((held, HEAD_SIZE), jnp.bfloat16),
            pltpu.VMEM((used, width), jnp.bfloat16),
            pltpu.VMEM((used, width), jnp.bfloat16),
            pltpu.VMEM((held, 2 * HEAD_SIZE), jnp.float32),
        ],
        compiler_params=pltpu.CompilerParams(vmem_limit_bytes=VMEM_LIMIT),
        cost_estimate=COST,
        name="backward",
    )(doc_ids, qt, q_rows, lse, *grads, *extra, *kvs)


def part_of(w_ref, which, part):
    me = lax.axis_index("tp") ^ which
    return w_ref[:, pl.ds(pl.multiple_of(me * part, BLK), part)]


def features_in_kernel(which, *refs):
    *cots, near_ref, w_ref, ot_ref, gt_ref, g_rows_ref, delta_ref = refs
    rows, part = cots[0].shape
    width = near_ref.shape[1]
    total = near_ref[...]
    for j, cot in zip(which, cots):
        total += lax.dot_general(
            cot[...], part_of(w_ref, j, part), (((1,), (1,)), ((), ())),
            preferred_element_type=jnp.float32,
        )
    grad = total.astype(jnp.bfloat16)
    for b in range(rows // BLK):
        for h in range(width // BLK):
            g = grad[b * BLK:(b + 1) * BLK, h * BLK:(h + 1) * BLK]
            g_rows_ref[pl.ds(b * width + h * BLK, BLK), :] = g
            gt_ref[block(b), block(h)] = g.T
        delta_ref[pl.ds(b, 1), :] = jnp.sum(
            gt_ref[block(b), :].astype(jnp.float32) * ot_ref[block(b), :].astype(jnp.float32),
            axis=0, keepdims=True,
        )


def features_in(which, cots, weight, near, ot):
    rows, width = near.shape
    blocks = rows // BLK
    return pl.pallas_call(
        functools.partial(features_in_kernel, which),
        out_shape=[
            jax.ShapeDtypeStruct((rows, width), jnp.bfloat16),
            jax.ShapeDtypeStruct((blocks * width, BLK), jnp.bfloat16),
            jax.ShapeDtypeStruct((blocks, width), jnp.float32),
        ],
        in_specs=[VMEM] * (len(cots) + 3),
        out_specs=[VMEM] * 3,
        compiler_params=pltpu.CompilerParams(vmem_limit_bytes=VMEM_LIMIT),
        cost_estimate=COST,
        name="features_in",
    )(*cots, near, weight, ot)


def features_out_kernel(which, attn_ref, *refs):
    *extra, w_ref, out_ref = refs
    total = dot(attn_ref[...], part_of(w_ref, which, out_ref.shape[1]))
    for ref in extra:
        total = total + ref[...].astype(jnp.float32)
    out_ref[...] = total.astype(out_ref.dtype)


def features_out(which, attn, weight, part, extra=(), dtype=jnp.bfloat16):
    rows, depth = attn.shape
    return pl.pallas_call(
        functools.partial(features_out_kernel, which),
        out_shape=jax.ShapeDtypeStruct((rows, part), dtype),
        in_specs=[VMEM] * (2 + len(extra)),
        out_specs=VMEM,
        compiler_params=pltpu.CompilerParams(vmem_limit_bytes=VMEM_LIMIT),
        cost_estimate=COST,
        name="features_out",
    )(attn, *extra, weight)


def join_kernel(k_hbm, v_hbm, whole_ref, last_ref, k, v, sems):
    copies = [
        pltpu.make_async_copy(k_hbm, k, sems.at[0]),
        pltpu.make_async_copy(v_hbm, v, sems.at[1]),
    ]
    for copy in copies:
        copy.start()
    for copy in copies:
        copy.wait()
    skipped = k.shape[0] - last_ref.shape[0]
    whole_ref[:, :HEAD_SIZE] = k[...]
    whole_ref[:, HEAD_SIZE:] = v[...]
    last_ref[:, :HEAD_SIZE] = k[skipped:, :]
    last_ref[:, HEAD_SIZE:] = v[skipped:, :]


def join(keys, values, last):
    rows, width = keys.shape
    return pl.pallas_call(
        join_kernel,
        out_shape=[jax.ShapeDtypeStruct((n, 2 * width), keys.dtype) for n in (rows, last)],
        in_specs=[HBM] * 2,
        out_specs=[VMEM] * 2,
        scratch_shapes=[pltpu.VMEM(keys.shape, keys.dtype)] * 2 + [pltpu.SemaphoreType.DMA((2,))],
        compiler_params=pltpu.CompilerParams(vmem_limit_bytes=VMEM_LIMIT),
        cost_estimate=COST,
        name="join",
    )(in_hbm(keys), in_hbm(values))


def prepare_kernel(
    q_hbm, cot_hbm, cot_c_ref, w_hbm, near_ref, w_ref, qt_ref, q_rows_ref, q_ref, cot_ref, sems
):
    part = cot_ref.shape[1]
    rows, width = q_ref.shape
    me = lax.axis_index("tp")
    pairs = [(q_hbm, q_ref), (cot_hbm, cot_ref)]
    for j in range(4):
        columns = pl.ds(pl.multiple_of((me ^ j) * part, BLK), part)
        pairs.append((w_hbm.at[:, columns], w_ref.at[:, columns]))
    copies = [pltpu.make_async_copy(*pair, sems.at[i]) for i, pair in enumerate(pairs)]
    for copy in copies:
        copy.start()
    copies[0].wait()
    for b in range(rows // BLK):
        for h in range(width // BLK):
            q = q_ref[block(b), block(h)]
            qt_ref[block(b), block(h)] = q.T
            q_rows_ref[pl.ds(b * width + h * BLK, BLK), :] = q
    copies[1].wait()
    for j, cot in ((0, cot_ref), (1, cot_c_ref)):
        copies[2 + j].wait()
        product = lax.dot_general(
            cot[...], part_of(w_ref, j, part), (((1,), (1,)), ((), ())),
            preferred_element_type=jnp.float32,
        )
        near_ref[...] = product if j == 0 else near_ref[...] + product
    copies[4].wait()
    copies[5].wait()


def prepare(q, cot, cot_c, weight):
    rows, width = q.shape
    blocks = rows // BLK
    return pl.pallas_call(
        prepare_kernel,
        out_shape=[
            jax.ShapeDtypeStruct((rows, width), jnp.float32),
            jax.ShapeDtypeStruct(weight.shape, weight.dtype),
            jax.ShapeDtypeStruct((rows, width), q.dtype),
            jax.ShapeDtypeStruct((blocks * width, BLK), q.dtype),
        ],
        in_specs=[HBM, HBM, VMEM, HBM],
        out_specs=[VMEM] * 4,
        scratch_shapes=[
            pltpu.VMEM(q.shape, q.dtype),
            pltpu.VMEM(cot.shape, cot.dtype),
            pltpu.SemaphoreType.DMA((6,)),
        ],
        compiler_params=pltpu.CompilerParams(vmem_limit_bytes=VMEM_LIMIT),
        cost_estimate=COST,
        name="prepare",
    )(in_hbm(q), in_hbm(cot), cot_c, in_hbm(weight))


def add_kernel(*refs):
    *in_refs, out_ref = refs
    rows = out_ref.shape[0]
    out_ref[...] = in_refs[0][...]
    for ref in in_refs[1:]:
        count = ref.shape[0]
        out_ref[pl.ds(rows - count, count), :] += ref[...].astype(jnp.float32)


def add_up(arrays, cost):
    return pl.pallas_call(
        add_kernel,
        out_shape=jax.ShapeDtypeStruct(arrays[0].shape, jnp.float32),
        in_specs=[VMEM] * len(arrays),
        out_specs=VMEM,
        compiler_params=pltpu.CompilerParams(vmem_limit_bytes=VMEM_LIMIT),
        cost_estimate=cost,
        name="add_up",
    )(*arrays)


def finish_kernel(out_ref, other_ref, own_ref, back_ref, mixed_hbm, dk_hbm, dv_hbm,
                  mixed, dk, dv, sems):
    half = mixed.shape[0] // 2
    copies = [pltpu.make_async_copy(dk, dk_hbm, sems.at[0])]
    copies.append(pltpu.make_async_copy(dv, dv_hbm, sems.at[1]))
    total = own_ref[...] + back_ref[...].astype(jnp.float32)
    dk[...] = total[:, :HEAD_SIZE].astype(dk.dtype)
    dv[...] = total[:, HEAD_SIZE:].astype(dv.dtype)
    copies[0].start()
    copies[1].start()
    for i in range(2):
        rows = pl.ds(i * half, half)
        mixed[rows, :] = (out_ref[rows, :] + other_ref[rows, :].astype(jnp.float32)).astype(
            mixed.dtype
        )
        copies.append(
            pltpu.make_async_copy(mixed.at[rows, :], mixed_hbm.at[rows, :], sems.at[2 + i])
        )
        copies[-1].start()
    for copy in copies:
        copy.wait()


def finish(out, other, own, back):
    rows = own.shape[0]
    kinds = [
        jax.ShapeDtypeStruct(out.shape, jnp.bfloat16),
        jax.ShapeDtypeStruct((rows, HEAD_SIZE), jnp.bfloat16),
        jax.ShapeDtypeStruct((rows, HEAD_SIZE), jnp.bfloat16),
    ]
    return pl.pallas_call(
        finish_kernel,
        out_shape=kinds,
        in_specs=[VMEM] * 4,
        out_specs=[HBM] * 3,
        scratch_shapes=[pltpu.VMEM(kind.shape, kind.dtype) for kind in kinds]
        + [pltpu.SemaphoreType.DMA((4,))],
        compiler_params=pltpu.CompilerParams(vmem_limit_bytes=VMEM_LIMIT),
        cost_estimate=COST,
        name="finish",
    )(out, other, own, back)


def on_device(queries, keys, values, out_weight, cotangent, doc_ids):
    rows = queries.shape[0]
    part = cotangent.shape[1]
    ctx_count = lax.axis_size("ctx")
    blocks = rows // BLK
    window = min(8 * blocks, blocks * ctx_count // 2)
    needs = []
    left = window - 1
    while left > 0:
        needs.append(min(left, blocks))
        left -= needs[-1]
    odd = lax.axis_index("ctx") % 2
    key_value, tail = join(keys, values, needs[-1] * BLK)
    key_value, tail, cot = lax.optimization_barrier((key_value, tail, cotangent))
    cot_y = swap(cot, 2)
    held = [key_value, None]
    held += [
        (shift if s % 2 else turn)(tail if n < blocks else key_value, "ctx", s)
        for s, n in enumerate(needs[1:], start=2)
    ]
    held[1] = swap(jnp.where(odd == 0, key_value, held[2]), 1, "ctx")
    near, weight, qt, q_rows = prepare(queries, cot, swap(cot, 1), out_weight)
    def places_of(shards):
        places = []
        for s in shards:
            top = window - 1 - (s - 1) * blocks if s > 0 else window - 1 + blocks
            places += range(top - (needs[s - 1] if s > 0 else blocks), top)
        return tuple(places)

    def part_back(shards, before, taken, last_part):
        return backward(
            doc_ids, qt, q_rows, lse, grads, before, taken,
            [held[s] for s in shards], jnp.bfloat16 if shards[0] else jnp.float32,
            places_of(shards), window, last_part,
        )

    shards = list(range(len(needs), 1, -1)) + [0]
    state = forward(
        doc_ids, qt, None, [held[s] for s in shards], places_of(shards), window, False, LONG
    )
    attn, ot, lse = forward(doc_ids, qt, state, [held[1]], places_of([1]), window, True, COST)
    attn, cot_y = lax.optimization_barrier((attn, cot_y))
    cot_d = swap(cot_y, 1)
    grads = features_in((2, 3), [cot_y, cot_d], weight, near, ot)
    out_a = features_out(3, attn, weight, part)

    out_b = features_out(2, attn, weight, part, [swap(out_a, 1)])
    from_y = swap(out_b, 2)
    most = list(range(len(needs), 2, -1))
    dq, *parts = part_back(most + [1], None, None, False)
    taken = swap(parts[-1], 1, "ctx")
    parts = dict(zip(most, parts))
    dq, parts[2] = part_back([2], dq, (taken, 1), False)
    dq, own = part_back([0], dq, (taken, 0), True)
    backs = {s: turn(parts[s], "ctx", -s) for s in range(2, len(held))}
    out_c = features_out(1, attn, weight, part)
    out_d = features_out(0, attn, weight, part, [swap(out_c, 1)], jnp.float32)
    own = add_up([own] + [backs[s] for s in most], SHORT)
    mixed, dk, dv = finish(out_d, from_y, own, backs[2])
    return (mixed, dq, dk, dv)


def solution(mesh):
    return jax.shard_map(
        on_device,
        mesh=mesh,
        in_specs=(
            P("ctx", "tp"),
            P("ctx", "tp"),
            P("ctx", "tp"),
            P("tp", None),
            P("ctx", "tp"),
            P(),
        ),
        out_specs=(P("ctx", "tp"), P("ctx", "tp"), P("ctx", "tp"), P("ctx", "tp")),
        check_vma=False,
    )
```

```python
import functools
import math

import jax
import jax.numpy as jnp
from jax import lax
from jax.experimental import pallas as pl
from jax.experimental.pallas import tpu as pltpu
from jax.sharding import PartitionSpec as P

HEAD_SIZE = 128
BLK = 128
SCALE = 1.0 / math.sqrt(HEAD_SIZE)
SCALE2 = SCALE * math.log2(math.e)
LOW = -1e30
HIGH = 1e30
VMEM_LIMIT = 16 * 1024 * 1024

PAD = 16

COST = pl.CostEstimate(flops=2**20, bytes_accessed=2**10, transcendentals=0)
LONG = pl.CostEstimate(flops=2**31, bytes_accessed=2**10, transcendentals=0)

SHORT = pl.CostEstimate(flops=1073741824, bytes_accessed=2**10, transcendentals=0)
HBM = pl.BlockSpec(memory_space=pltpu.HBM)
VMEM = pl.BlockSpec(memory_space=pltpu.VMEM)
SMEM = pl.BlockSpec(memory_space=pltpu.SMEM)


def in_hbm(array):
    return pltpu.with_memory_space_constraint(array, pltpu.HBM)


def dot(a, b):
    return jnp.dot(a, b, preferred_element_type=jnp.float32)


def shift(array, axis, by):
    devices = lax.axis_size(axis)
    pairs = [(i, i + by) for i in range(devices) if 0 <= i + by < devices]
    return lax.ppermute(array, axis, pairs)


def turn(array, axis, by):
    devices = lax.axis_size(axis)
    return lax.ppermute(array, axis, [(i, (i + by) % devices) for i in range(devices)])


def swap(array, bit, axis="tp"):
    return lax.ppermute(array, axis, [(i, i ^ bit) for i in range(lax.axis_size(axis))])


def block(i, n=1):
    return pl.ds(i * BLK, n * BLK)


def allowed(doc_ref, key_block, query_block):
    return (key_block >= 0) & (doc_ref[jnp.maximum(key_block, 0)] == doc_ref[query_block])


def causal(width):
    key = lax.broadcasted_iota(jnp.int32, (BLK, width), 0)
    query = lax.broadcasted_iota(jnp.int32, (BLK, width), 1) % BLK
    return key <= query


def forward_kernel(window, blocks, places, first_part, last_part, doc_ref, qt_ref, *refs):
    refs = list(refs)
    before = None if first_part else [refs.pop(0) for _ in range(3)]
    kv_refs = refs[:-7]
    *out_refs, k_all, vt_all, s_all, p_all = refs[-7:]
    width = qt_ref.shape[1]
    heads = width // HEAD_SIZE
    first = lax.axis_index("ctx") * blocks
    at = 0
    for ref in kv_refs:
        rows = ref.shape[0] // BLK * BLK
        k_all[pl.ds(at, rows), :] = ref[:rows, :HEAD_SIZE]
        vt_all[:, pl.ds(at, rows)] = ref[:rows, HEAD_SIZE:].T
        at += rows
    for b in range(blocks):
        qt = qt_ref[block(b), :]
        if first_part:
            out, top, total = None, jnp.full((1, width), LOW, jnp.float32), None
        else:
            out, top, total = before[0][block(b), :], *(r[pl.ds(b, 1), :] for r in before[1:])
        earlier = top
        inside = [i for i, place in enumerate(places) if b <= place < b + window]
        start, stop = inside[0], inside[-1] + 1
        ok = {i: allowed(doc_ref, first - (window - 1) + places[i], first + b) for i in inside}
        for i in inside:
            s = dot(k_all[block(i), :], qt) * SCALE2
            if places[i] == b + window - 1:
                s = jnp.where(causal(width), s, LOW)
            s_all[block(i - start), :] = s
            top = jnp.maximum(top, jnp.max(s, axis=0, keepdims=True) + jnp.where(ok[i], 0.0, LOW))
        sums = jnp.zeros((1, width), jnp.float32)
        for i in inside:
            p = jnp.exp2(s_all[block(i - start), :] - jnp.where(ok[i], top, HIGH))
            sums += jnp.sum(p, axis=0, keepdims=True)
            p_all[block(i - start), :] = p.astype(jnp.bfloat16)
        fresh = dot(vt_all[:, block(start, stop - start)], p_all[block(0, stop - start), :])
        if first_part:
            out, total = fresh, sums
        else:
            factor = jnp.exp2(earlier - top)
            out, total = out * factor + fresh, total * factor + sums
        if last_part:
            attn_ref, ot_ref, lse_ref = out_refs
            out = (out / total).astype(jnp.bfloat16)
            ot_ref[block(b), :] = out
            lse_ref[pl.ds(b, 1), :] = top + jnp.log2(total)
            for h in range(heads):
                attn_ref[block(b), block(h)] = out[:, h * BLK:(h + 1) * BLK].T
        else:
            out_ref, top_ref, total_ref = out_refs
            out_ref[block(b), :] = out
            top_ref[pl.ds(b, 1), :] = top
            total_ref[pl.ds(b, 1), :] = total


def forward(doc_ids, qt, before, kvs, places, window, last_part, cost):
    rows, width = qt.shape
    blocks = rows // BLK
    held = len(places) * BLK
    used = min(held, window * BLK)
    extra = [] if before is None else list(before)
    stats = jax.ShapeDtypeStruct((blocks, width), jnp.float32)
    if last_part:
        out_shape = [jax.ShapeDtypeStruct((rows, width), jnp.bfloat16)] * 2 + [stats]
    else:
        out_shape = [jax.ShapeDtypeStruct((rows, width), jnp.float32), stats, stats]
    return pl.pallas_call(
        functools.partial(forward_kernel, window, blocks, places, before is None, last_part),
        out_shape=out_shape,
        in_specs=[SMEM] + [VMEM] * (1 + len(extra) + len(kvs)),
        out_specs=[VMEM] * 3,
        scratch_shapes=[
            pltpu.VMEM((held, HEAD_SIZE), jnp.bfloat16),
            pltpu.VMEM((HEAD_SIZE, held), jnp.bfloat16),
            pltpu.VMEM((used, width), jnp.float32),
            pltpu.VMEM((used, width), jnp.bfloat16),
        ],
        compiler_params=pltpu.CompilerParams(vmem_limit_bytes=VMEM_LIMIT),
        cost_estimate=cost,
        name="forward",
    )(doc_ids, qt, *extra, *kvs)


def backward_kernel(
    window, blocks, places, first_part, last_part, taking,
    doc_ref, qt_ref, q_rows_ref, lse_ref, gt_ref, g_rows_ref, delta_ref, *refs
):
    refs = list(refs)
    before_ref = None if first_part else refs.pop(0)
    taken_ref = None if taking is None else refs.pop(0)
    n = (len(refs) - 7) // 2
    kv_refs, dq_ref, dkv_refs = refs[:n], refs[n], refs[n + 1:2 * n + 1]
    k_all, kt_all, v_all, p_all, ds_all, dkv_all = refs[2 * n + 1:]
    width = qt_ref.shape[1]
    heads = width // HEAD_SIZE
    me = lax.axis_index("ctx")
    first = me * blocks
    at = 0
    for ref in kv_refs:
        rows = ref.shape[0] // BLK * BLK
        k_all[pl.ds(at, rows), :] = ref[:rows, :HEAD_SIZE]
        kt_all[:, pl.ds(at, rows)] = ref[:rows, :HEAD_SIZE].T
        v_all[pl.ds(at, rows), :] = ref[:rows, HEAD_SIZE:]
        at += rows
    dkv_all[...] = jnp.zeros_like(dkv_all)
    for b in range(blocks):
        qt, gt = qt_ref[block(b), :], gt_ref[block(b), :]
        delta = delta_ref[pl.ds(b, 1), :]
        lse = lse_ref[pl.ds(b, 1), :]
        inside = [i for i, place in enumerate(places) if b <= place < b + window]
        if not inside:
            if first_part:
                dq_ref[block(b), :] = jnp.zeros((BLK, width), jnp.float32)
            else:
                dq_ref[block(b), :] = before_ref[block(b), :]
            continue
        start, stop = inside[0], inside[-1] + 1
        for i in inside:
            ok = allowed(doc_ref, first - (window - 1) + places[i], first + b)
            s = dot(k_all[block(i), :], qt) * SCALE2
            if places[i] == b + window - 1:
                s = jnp.where(causal(width), s, LOW)
            p = jnp.exp2(s - jnp.where(ok, lse, HIGH))
            p_all[block(i - start), :] = p.astype(jnp.bfloat16)
            dp = dot(v_all[block(i), :], gt)
            ds_all[block(i - start), :] = (p * (dp - delta)).astype(jnp.bfloat16)
        mine, used = block(start, stop - start), block(0, stop - start)
        stacked = pl.ds(b * width, width)
        dkv_all[mine, :HEAD_SIZE] += dot(ds_all[used, :], q_rows_ref[stacked, :]) * SCALE
        dkv_all[mine, HEAD_SIZE:] += dot(p_all[used, :], g_rows_ref[stacked, :])
        dqt = dot(kt_all[:, mine], ds_all[used, :]) * SCALE
        if not first_part:
            dqt += before_ref[block(b), :]
        if last_part:
            dqt = dqt.astype(jnp.bfloat16)
            for h in range(heads):
                dq_ref[block(b), block(h)] = dqt[:, h * BLK:(h + 1) * BLK].T
        else:
            dq_ref[block(b), :] = dqt
    at = 0
    for ref in dkv_refs:
        rows = ref.shape[0]
        total = dkv_all[pl.ds(at, rows), :]
        at += rows
        if taken_ref is not None and ref is dkv_refs[-1]:
            total += jnp.where(me % 2 == taking, taken_ref[...].astype(jnp.float32), 0.0)
        ref[...] = total.astype(ref.dtype)


def backward(doc_ids, qt, q_rows, lse, grads, before, taken, kvs, kind, places, window, last_part):
    rows, width = qt.shape
    blocks = rows // BLK
    held = len(places) * BLK
    used = min(held, window * BLK)
    extra = [] if before is None else [before]
    extra += [] if taken is None else [taken[0]]
    dq_kind = jnp.bfloat16 if last_part else jnp.float32
    return pl.pallas_call(
        functools.partial(
            backward_kernel, window, blocks, places, before is None, last_part,
            None if taken is None else taken[1],
        ),
        out_shape=[jax.ShapeDtypeStruct((rows, width), dq_kind)]
        + [jax.ShapeDtypeStruct((kv.shape[0] // BLK * BLK, kv.shape[1]), kind) for kv in kvs],
        in_specs=[SMEM] + [VMEM] * (6 + len(extra) + len(kvs)),
        out_specs=[VMEM] * (1 + len(kvs)),
        scratch_shapes=[
            pltpu.VMEM((held, HEAD_SIZE), jnp.bfloat16),
            pltpu.VMEM((HEAD_SIZE, held), jnp.bfloat16),
            pltpu.VMEM((held, HEAD_SIZE), jnp.bfloat16),
            pltpu.VMEM((used, width), jnp.bfloat16),
            pltpu.VMEM((used, width), jnp.bfloat16),
            pltpu.VMEM((held, 2 * HEAD_SIZE), jnp.float32),
        ],
        compiler_params=pltpu.CompilerParams(vmem_limit_bytes=VMEM_LIMIT),
        cost_estimate=COST,
        name="backward",
    )(doc_ids, qt, q_rows, lse, *grads, *extra, *kvs)


def part_of(w_ref, which, part):
    me = lax.axis_index("tp") ^ which
    return w_ref[:, pl.ds(pl.multiple_of(me * part, BLK), part)]


def features_in_kernel(which, *refs):
    *cots, near_ref, w_ref, ot_ref, gt_ref, g_rows_ref, delta_ref = refs
    rows, part = cots[0].shape
    width = near_ref.shape[1]
    total = near_ref[...]
    for j, cot in zip(which, cots):
        total += lax.dot_general(
            cot[...], part_of(w_ref, j, part), (((1,), (1,)), ((), ())),
            preferred_element_type=jnp.float32,
        )
    grad = total.astype(jnp.bfloat16)
    for b in range(rows // BLK):
        for h in range(width // BLK):
            g = grad[b * BLK:(b + 1) * BLK, h * BLK:(h + 1) * BLK]
            g_rows_ref[pl.ds(b * width + h * BLK, BLK), :] = g
            gt_ref[block(b), block(h)] = g.T
        delta_ref[pl.ds(b, 1), :] = jnp.sum(
            gt_ref[block(b), :].astype(jnp.float32) * ot_ref[block(b), :].astype(jnp.float32),
            axis=0, keepdims=True,
        )


def features_in(which, cots, weight, near, ot):
    rows, width = near.shape
    blocks = rows // BLK
    return pl.pallas_call(
        functools.partial(features_in_kernel, which),
        out_shape=[
            jax.ShapeDtypeStruct((rows, width), jnp.bfloat16),
            jax.ShapeDtypeStruct((blocks * width, BLK), jnp.bfloat16),
            jax.ShapeDtypeStruct((blocks, width), jnp.float32),
        ],
        in_specs=[VMEM] * (len(cots) + 3),
        out_specs=[VMEM] * 3,
        compiler_params=pltpu.CompilerParams(vmem_limit_bytes=VMEM_LIMIT),
        cost_estimate=COST,
        name="features_in",
    )(*cots, near, weight, ot)


def features_out_kernel(which, attn_ref, *refs):
    *extra, w_ref, out_ref = refs
    total = dot(attn_ref[...], part_of(w_ref, which, out_ref.shape[1]))
    for ref in extra:
        total = total + ref[...].astype(jnp.float32)
    out_ref[...] = total.astype(out_ref.dtype)


def features_out(which, attn, weight, part, extra=(), dtype=jnp.bfloat16):
    rows, depth = attn.shape
    return pl.pallas_call(
        functools.partial(features_out_kernel, which),
        out_shape=jax.ShapeDtypeStruct((rows, part), dtype),
        in_specs=[VMEM] * (2 + len(extra)),
        out_specs=VMEM,
        compiler_params=pltpu.CompilerParams(vmem_limit_bytes=VMEM_LIMIT),
        cost_estimate=COST,
        name="features_out",
    )(attn, *extra, weight)


def join_kernel(k_hbm, v_hbm, whole_ref, last_ref, padded_ref, k, v, sems):
    copies = [
        pltpu.make_async_copy(k_hbm, k, sems.at[0]),
        pltpu.make_async_copy(v_hbm, v, sems.at[1]),
    ]
    for copy in copies:
        copy.start()
    for copy in copies:
        copy.wait()
    skipped = k.shape[0] - last_ref.shape[0]
    whole_ref[:, :HEAD_SIZE] = k[...]
    whole_ref[:, HEAD_SIZE:] = v[...]
    last_ref[:, :HEAD_SIZE] = k[skipped:, :]
    last_ref[:, HEAD_SIZE:] = v[skipped:, :]
    padded_ref[:k.shape[0], :] = whole_ref[...]
    padded_ref[k.shape[0]:, :] = jnp.zeros_like(padded_ref[k.shape[0]:, :])


def join(keys, values, last):
    rows, width = keys.shape
    return pl.pallas_call(
        join_kernel,
        out_shape=[jax.ShapeDtypeStruct((n, 2 * width), keys.dtype) for n in (rows, last, rows + PAD)],
        in_specs=[HBM] * 2,
        out_specs=[VMEM] * 3,
        scratch_shapes=[pltpu.VMEM(keys.shape, keys.dtype)] * 2 + [pltpu.SemaphoreType.DMA((2,))],
        compiler_params=pltpu.CompilerParams(vmem_limit_bytes=VMEM_LIMIT),
        cost_estimate=COST,
        name="join",
    )(in_hbm(keys), in_hbm(values))


def prepare_kernel(
    q_hbm, cot_hbm, cot_c_ref, w_hbm, near_ref, w_ref, qt_ref, q_rows_ref, q_ref, cot_ref, sems
):
    part = cot_ref.shape[1]
    rows, width = q_ref.shape
    me = lax.axis_index("tp")
    pairs = [(q_hbm, q_ref), (cot_hbm, cot_ref)]
    for j in range(4):
        columns = pl.ds(pl.multiple_of((me ^ j) * part, BLK), part)
        pairs.append((w_hbm.at[:, columns], w_ref.at[:, columns]))
    copies = [pltpu.make_async_copy(*pair, sems.at[i]) for i, pair in enumerate(pairs)]
    for copy in copies:
        copy.start()
    copies[0].wait()
    for b in range(rows // BLK):
        for h in range(width // BLK):
            q = q_ref[block(b), block(h)]
            qt_ref[block(b), block(h)] = q.T
            q_rows_ref[pl.ds(b * width + h * BLK, BLK), :] = q
    copies[1].wait()
    for j, cot in ((0, cot_ref), (1, cot_c_ref)):
        copies[2 + j].wait()
        product = lax.dot_general(
            cot[...], part_of(w_ref, j, part), (((1,), (1,)), ((), ())),
            preferred_element_type=jnp.float32,
        )
        near_ref[...] = product if j == 0 else near_ref[...] + product
    copies[4].wait()
    copies[5].wait()


def prepare(q, cot, cot_c, weight):
    rows, width = q.shape
    blocks = rows // BLK
    return pl.pallas_call(
        prepare_kernel,
        out_shape=[
            jax.ShapeDtypeStruct((rows, width), jnp.float32),
            jax.ShapeDtypeStruct(weight.shape, weight.dtype),
            jax.ShapeDtypeStruct((rows, width), q.dtype),
            jax.ShapeDtypeStruct((blocks * width, BLK), q.dtype),
        ],
        in_specs=[HBM, HBM, VMEM, HBM],
        out_specs=[VMEM] * 4,
        scratch_shapes=[
            pltpu.VMEM(q.shape, q.dtype),
            pltpu.VMEM(cot.shape, cot.dtype),
            pltpu.SemaphoreType.DMA((6,)),
        ],
        compiler_params=pltpu.CompilerParams(vmem_limit_bytes=VMEM_LIMIT),
        cost_estimate=COST,
        name="prepare",
    )(in_hbm(q), in_hbm(cot), cot_c, in_hbm(weight))


def add_kernel(*refs):
    *in_refs, out_ref = refs
    rows = out_ref.shape[0]
    out_ref[...] = in_refs[0][...]
    for ref in in_refs[1:]:
        count = ref.shape[0]
        out_ref[pl.ds(rows - count, count), :] += ref[...].astype(jnp.float32)


def add_up(arrays, cost):
    return pl.pallas_call(
        add_kernel,
        out_shape=jax.ShapeDtypeStruct(arrays[0].shape, jnp.float32),
        in_specs=[VMEM] * len(arrays),
        out_specs=VMEM,
        compiler_params=pltpu.CompilerParams(vmem_limit_bytes=VMEM_LIMIT),
        cost_estimate=cost,
        name="add_up",
    )(*arrays)


def finish_kernel(out_ref, other_ref, own_ref, back_ref, mixed_hbm, dk_hbm, dv_hbm,
                  mixed, dk, dv, sems):
    half = mixed.shape[0] // 2
    copies = [pltpu.make_async_copy(dk, dk_hbm, sems.at[0])]
    copies.append(pltpu.make_async_copy(dv, dv_hbm, sems.at[1]))
    total = own_ref[...] + back_ref[...].astype(jnp.float32)
    dk[...] = total[:, :HEAD_SIZE].astype(dk.dtype)
    dv[...] = total[:, HEAD_SIZE:].astype(dv.dtype)
    copies[0].start()
    copies[1].start()
    for i in range(2):
        rows = pl.ds(i * half, half)
        mixed[rows, :] = (out_ref[rows, :] + other_ref[rows, :].astype(jnp.float32)).astype(
            mixed.dtype
        )
        copies.append(
            pltpu.make_async_copy(mixed.at[rows, :], mixed_hbm.at[rows, :], sems.at[2 + i])
        )
        copies[-1].start()
    for copy in copies:
        copy.wait()


def finish(out, other, own, back):
    rows = own.shape[0]
    kinds = [
        jax.ShapeDtypeStruct(out.shape, jnp.bfloat16),
        jax.ShapeDtypeStruct((rows, HEAD_SIZE), jnp.bfloat16),
        jax.ShapeDtypeStruct((rows, HEAD_SIZE), jnp.bfloat16),
    ]
    return pl.pallas_call(
        finish_kernel,
        out_shape=kinds,
        in_specs=[VMEM] * 4,
        out_specs=[HBM] * 3,
        scratch_shapes=[pltpu.VMEM(kind.shape, kind.dtype) for kind in kinds]
        + [pltpu.SemaphoreType.DMA((4,))],
        compiler_params=pltpu.CompilerParams(vmem_limit_bytes=VMEM_LIMIT),
        cost_estimate=COST,
        name="finish",
    )(out, other, own, back)


def on_device(queries, keys, values, out_weight, cotangent, doc_ids):
    rows = queries.shape[0]
    part = cotangent.shape[1]
    ctx_count = lax.axis_size("ctx")
    blocks = rows // BLK
    window = min(8 * blocks, blocks * ctx_count // 2)
    needs = []
    left = window - 1
    while left > 0:
        needs.append(min(left, blocks))
        left -= needs[-1]
    odd = lax.axis_index("ctx") % 2
    key_value, tail, padded = join(keys, values, needs[-1] * BLK)
    key_value, tail, padded, cot = lax.optimization_barrier((key_value, tail, padded, cotangent))
    cot_y = swap(cot, 2)
    held = [key_value, None]
    held += [
        shift(padded, "ctx", s) if s % 2 else turn(tail if n < blocks else key_value, "ctx", s)
        for s, n in enumerate(needs[1:], start=2)
    ]
    held[1] = swap(jnp.where(odd == 0, key_value, held[2]), 1, "ctx")
    near, weight, qt, q_rows = prepare(queries, cot, swap(cot, 1), out_weight)
    def places_of(shards):
        places = []
        for s in shards:
            top = window - 1 - (s - 1) * blocks if s > 0 else window - 1 + blocks
            places += range(top - (needs[s - 1] if s > 0 else blocks), top)
        return tuple(places)

    def part_back(shards, before, taken, last_part):
        return backward(
            doc_ids, qt, q_rows, lse, grads, before, taken,
            [held[s] for s in shards], jnp.bfloat16 if shards[0] else jnp.float32,
            places_of(shards), window, last_part,
        )

    shards = list(range(len(needs), 1, -1)) + [0]
    state = forward(
        doc_ids, qt, None, [held[s] for s in shards], places_of(shards), window, False, LONG
    )
    attn, ot, lse = forward(doc_ids, qt, state, [held[1]], places_of([1]), window, True, COST)
    attn, cot_y = lax.optimization_barrier((attn, cot_y))
    cot_d = swap(cot_y, 1)
    grads = features_in((2, 3), [cot_y, cot_d], weight, near, ot)
    out_a = features_out(3, attn, weight, part)

    out_b = features_out(2, attn, weight, part, [swap(out_a, 1)])
    from_y = swap(out_b, 2)
    most = list(range(len(needs), 2, -1))
    dq, *parts = part_back(most + [1], None, None, False)
    taken = swap(parts[-1], 1, "ctx")
    parts = dict(zip(most, parts))
    dq, parts[2] = part_back([2], dq, (taken, 1), False)
    dq, own = part_back([0], dq, (taken, 0), True)
    backs = {s: turn(parts[s], "ctx", -s) for s in range(2, len(held))}
    out_c = features_out(1, attn, weight, part)
    out_d = features_out(0, attn, weight, part, [swap(out_c, 1)], jnp.float32)
    own = add_up([own] + [backs[s] for s in most], SHORT)
    mixed, dk, dv = finish(out_d, from_y, own, backs[2])
    return (mixed, dq, dk, dv)


def solution(mesh):
    return jax.shard_map(
        on_device,
        mesh=mesh,
        in_specs=(
            P("ctx", "tp"),
            P("ctx", "tp"),
            P("ctx", "tp"),
            P("tp", None),
            P("ctx", "tp"),
            P(),
        ),
        out_specs=(P("ctx", "tp"), P("ctx", "tp"), P("ctx", "tp"), P("ctx", "tp")),
        check_vma=False,
    )
```
